1024 devices in a mesh: ep: 16 (over x, z_hi), edp: 64 (over z_lo, y, core).
Axes of the slice: x: 8, y: 8, z: 8 (z_hi: 2, z_lo: 4; z = z_hi * 4 + z_lo), core: 2. Of those that a mesh axis runs over, the one named last changes fastest.
Arguments:
- tokens: bfloat16 [2048, 4096], P('ep', 'edp'), may hold values from -6 to 6
- out_grad: bfloat16 [2048, 4096], P('ep', 'edp'), may hold values from -1.5 to 1.5
- probs: float32 [2048, 8], P('ep'), may hold values from 0.1 to 1
- expert_ids: int32 [2048, 8], P('ep'), may hold values from 0 to 127, all different within a row; in each aligned block of 128 rows (0 to 127, 128 to 255, ...) at most 16 rows name the same one
- w_gate: bfloat16 [64, 4096, 1024], P('edp', 'ep'), may hold values from -0.09375 to 0.09375
- w_up: bfloat16 [64, 4096, 1024], P('edp', 'ep'), may hold values from -0.09375 to 0.09375
- w_down: bfloat16 [64, 1024, 4096], P('edp', None, 'ep'), may hold values from -0.1875 to 0.1875
Outputs:
- token_grad: bfloat16 [2048, 4096], P('ep', 'edp')
- grad_gate: bfloat16 [64, 4096, 1024], P('edp', 'ep')
- grad_up: bfloat16 [64, 4096, 1024], P('edp', 'ep')
- grad_down: bfloat16 [64, 1024, 4096], P('edp', None, 'ep')
The draws below stay inside these ranges and needn't reach their ends.
Inputs may be any that keep to these rules, and one draw needn't show every extreme that they name: `expert_ids`: each row names 8 different experts; within each context block of 128 tokens no expert is named by more than 16 tokens, a bound that some block reaches.
All inputs are finite; a program needn't handle non-finite values.
Results may differ from the reference program's by a relative error of at most 0.0058.
Values may be sent and summed in bfloat16 or wider, within the bound.
No kernel may reach another device: no remote copies, remote signals or barrier semaphores. Data moves between devices by JAX's collectives and lax.ppermute only.
A program may use at most 32 MiB of HBM per device.

```python
import math
import jax
import jax.numpy as jnp
import numpy as np
from jax import lax

D = 4096
EXPERTS = 128
TOP = 8
HID = 1024
TOK_CTX = 128
CAP = 16
TOKENS = 2048
EWIN = 64


def levels(rng, shape, cuts, low, largest):
    def one(axis_at, parts):
        draws = jax.random.uniform(jax.random.fold_in(jax.random.fold_in(rng, 6), axis_at), (parts,), jnp.float32, low / len(cuts), largest / len(cuts))
        return jnp.repeat(jnp.exp(draws), shape[axis_at] // parts).reshape((-1,) + (1,) * (len(shape) - axis_at - 1))

    loudness = one(*cuts[0])
    for cut in cuts[1:]:
        loudness = loudness * one(*cut)
    return loudness


def shared_out(key, own, number, rows, number_of, top, bound, skew):
    order = jax.random.permutation(key, number_of)
    heavy_load, usual = load_shares(number_of, rows * top, bound, skew, True), load_shares(number_of, rows * top, bound, skew, False)
    places = jnp.arange(number_of)

    def named(tallies, offset_by):
        used = int((tallies > 0).sum())
        fixed = max(1, used // 4)
        shifted = fixed + (places - fixed + offset_by * (used - fixed)) % max(1, number_of - fixed)
        return jnp.zeros((number_of,), jnp.int32).at[order[jnp.where(places < fixed, places, shifted)]].set(jnp.asarray(tallies, jnp.int32))

    tallies = jnp.where(number % 4 == 0, named(heavy_load, number // 4), named(usual, number - number // 4 - 1))
    mixed = jax.random.permutation(jax.random.fold_in(own, 3), number_of)
    giver, sink = mixed[0:number_of // 2 * 2:2], mixed[1:number_of // 2 * 2:2]
    margin = jnp.minimum(tallies[giver] - 1, bound - tallies[sink]) // 2
    margin = jnp.where((giver == order[0]) | (sink == order[0]) | (tallies[sink] == 0), 0, jnp.maximum(margin, 0))
    shifted = jax.random.randint(jax.random.fold_in(own, 4), (number_of // 2,), 0, 1 << 20) % (margin + 1)
    tallies = tallies.at[giver].add(-shifted).at[sink].add(shifted)
    labels = jnp.searchsorted(jnp.cumsum(tallies), jnp.arange(rows * top), side="right").astype(jnp.int32)
    table = labels.reshape(top, rows).T
    table = table[jax.random.permutation(jax.random.fold_in(own, 1), rows)]
    offset_by = jax.random.randint(jax.random.fold_in(own, 2), (rows, 1), 0, top)
    return jnp.take_along_axis(table, (jnp.arange(top)[None, :] + offset_by) % top, axis=1)


def load_shares(amount, total, limit, skew, full):
    weights = [(1 << 20) // math.isqrt(rank ** skew) + 1 for rank in range(1, amount + 1)]
    largest = limit if full else min(limit, max(-(-total // amount), total * weights[0] // sum(weights)))
    least = 1 if total - largest >= amount - 1 else 0
    given, surplus = [largest] + [least] * (amount - 1), total - largest - least * (amount - 1)
    while surplus > 0:
        movable = [i for i in range(1, amount) if given[i] < largest] or [i for i in range(1, amount) if given[i] < limit]
        pool, remaining = sum([weights[i] for i in movable]), surplus
        for i in movable:
            addition = min(limit - given[i], max(1, remaining * weights[i] // pool), surplus)
            given[i] = given[i] + addition
            surplus = surplus - addition
    return np.array(given)


def gaussian(stream_key, dims, spread, limit, pieces=(), kind=jnp.bfloat16):
    entries = jax.random.normal(stream_key, dims, jnp.float32) * spread
    if len(pieces) > 0:
        entries = levels(stream_key, dims, pieces, -0.22, 0.18) * entries
    return jnp.clip(entries, min=-limit, max=limit).astype(kind)


def setup_inputs(seed: int = 0) -> dict:
    seeds = jax.random.split(jax.random.key(seed), 8)
    tokens = gaussian(seeds[0], (TOKENS, D), 1.0, 6.0, ((0, 16), (1, 64)))
    out_grad = gaussian(seeds[1], (TOKENS, D), 0.25, 1.5, ((0, 16), (1, 64)))
    probs = jnp.clip(0.1 + 0.9 * jax.random.uniform(seeds[2], (TOKENS, TOP), jnp.float32) ** levels(seeds[2], (TOKENS, TOP), ((0, 16),), -0.2, 0.2), 0.1, 1.0)
    expert_ids_keys = jax.random.split(jax.random.fold_in(seeds[3], 1), TOKENS // TOK_CTX)
    expert_ids_turns = jax.random.permutation(jax.random.fold_in(seeds[3], 3), TOKENS // TOK_CTX)
    expert_ids = jax.vmap(lambda own, number: shared_out(jax.random.fold_in(seeds[3], 2), own, number, TOK_CTX, EXPERTS, TOP, CAP, 2))(expert_ids_keys, expert_ids_turns).reshape((TOKENS, TOP))
    w_gate = gaussian(seeds[4], (EWIN, D, HID), D ** -0.5, 0.09375, ((0, 64), (1, 16)))
    w_up = gaussian(seeds[5], (EWIN, D, HID), D ** -0.5, 0.09375, ((0, 64), (1, 16)))
    w_down = gaussian(seeds[6], (EWIN, HID, D), HID ** -0.5, 0.1875, ((0, 64), (2, 16)))
    return {"tokens": tokens, "out_grad": out_grad, "probs": probs, "expert_ids": expert_ids, "w_gate": w_gate, "w_up": w_up, "w_down": w_down}


def reference(tokens, out_grad, probs, expert_ids, w_gate, w_up, w_down):
    blocks = TOKENS // TOK_CTX
    slot_rows = blocks * CAP
    pick_count = TOK_CTX * TOP
    chosen_ids = expert_ids.reshape(blocks, pick_count)
    weights = probs.reshape(blocks, pick_count)
    token_index = (jnp.arange(blocks, dtype=jnp.int32)[:, None] * TOK_CTX
                   + jnp.arange(pick_count, dtype=jnp.int32)[None, :] // TOP)
    block_base = jnp.arange(blocks, dtype=jnp.int32)[:, None] * CAP

    def per_expert(running, expert):
        chosen = (chosen_ids == expert).astype(jnp.int32)
        ranking = jnp.cumsum(chosen, axis=1) - chosen
        target = jnp.where(chosen > 0, block_base + ranking, slot_rows).reshape(-1).astype(jnp.int32)
        token_table = jnp.zeros((slot_rows,), jnp.int32).at[target].set(token_index.reshape(-1), mode="drop")
        slot_weight = jnp.zeros((slot_rows,), jnp.float32).at[target].set(weights.reshape(-1), mode="drop")
        filled = jnp.zeros((slot_rows,), jnp.int32).at[target].set(1, mode="drop")
        occupied = (filled > 0)[:, None]
        slot_tokens = jnp.where(occupied, tokens[token_table], jnp.zeros((), tokens.dtype))
        slot_grads = jnp.where(occupied, out_grad[token_table], jnp.zeros((), out_grad.dtype))
        gate_local = w_gate[expert]
        up_local = w_up[expert]
        down_local = w_down[expert]
        gate_sum = jnp.dot(slot_tokens, gate_local, preferred_element_type=jnp.float32)
        up_sum = jnp.dot(slot_tokens, up_local, preferred_element_type=jnp.float32)
        back_sum = jnp.dot(slot_grads, down_local.T, preferred_element_type=jnp.float32)
        weight_col = slot_weight[:, None]
        sigmoid_gate = jax.nn.sigmoid(gate_sum)
        silu_gate = gate_sum * sigmoid_gate
        hidden_grad = weight_col * back_sum
        hidden_weighted = (weight_col * silu_gate * up_sum).astype(jnp.bfloat16)
        up_grad = (hidden_grad * silu_gate).astype(jnp.bfloat16)
        gate_grad = (hidden_grad * up_sum * sigmoid_gate * (1.0 + gate_sum * (1.0 - sigmoid_gate))).astype(jnp.bfloat16)
        slot_grad = (jnp.dot(gate_grad, gate_local.T, preferred_element_type=jnp.float32)
                     + jnp.dot(up_grad, up_local.T, preferred_element_type=jnp.float32)).astype(jnp.bfloat16)
        running = running.at[token_table].add(jnp.where(occupied, slot_grad.astype(jnp.float32), 0.0))
        grad_gate = jnp.dot(slot_tokens.T, gate_grad, preferred_element_type=jnp.float32).astype(jnp.bfloat16)
        grad_up = jnp.dot(slot_tokens.T, up_grad, preferred_element_type=jnp.float32).astype(jnp.bfloat16)
        grad_down = jnp.dot(hidden_weighted.T, slot_grads, preferred_element_type=jnp.float32).astype(jnp.bfloat16)
        return running, (grad_gate, grad_up, grad_down)

    running, grads = lax.scan(per_expert, jnp.zeros((TOKENS, D), jnp.float32), jnp.arange(EWIN, dtype=jnp.int32))
    return running.astype(jnp.bfloat16), grads[0], grads[1], grads[2]
```

```python
import jax
import jax.numpy as jnp
from jax import lax
from jax.experimental import pallas as pl
from jax.experimental.pallas import tpu as pltpu
from jax.sharding import PartitionSpec as P

CAP = 16
BF16 = jnp.bfloat16
F32 = jnp.float32
LAST = (((1,), (1,)), ((), ()))
FIRST = (((0,), (0,)), ((), ()))


def call(body, outs, flops, moved, *args):
    return pl.pallas_call(
        body,
        out_shape=outs,
        compiler_params=pltpu.CompilerParams(vmem_limit_bytes=40 * 1024 * 1024),
        cost_estimate=pl.CostEstimate(flops=flops, bytes_accessed=moved, transcendentals=0),
    )(*args)


def arr(shape, dtype=BF16):
    return jax.ShapeDtypeStruct(shape, dtype)


def before(toks):
    row = lax.broadcasted_iota(jnp.int32, (toks, toks), 0)
    col = lax.broadcasted_iota(jnp.int32, (toks, toks), 1)
    return jnp.where(row < col, 1.0, 0.0).astype(BF16)


def dispatch_body(experts, packed_ref, sent_ref, disp_ref):
    feats = packed_ref[0:128, :]
    ids = packed_ref[128:144, :].astype(F32)
    toks = ids.shape[1]
    names = lax.broadcasted_iota(jnp.int32, (experts, toks), 0).astype(F32)
    mask = jnp.zeros((experts, toks), F32)
    for k in range(8):
        mask = mask + jnp.where(ids[k : k + 1, :] == names, 1.0, 0.0)
    rank = jnp.dot(mask.astype(BF16), before(toks), preferred_element_type=F32)
    slot = jnp.where(mask > 0.0, rank, -1.0)
    place = lax.broadcasted_iota(jnp.int32, (CAP, toks), 0).astype(F32)
    for e in range(experts):
        disp_ref[e * CAP : (e + 1) * CAP, :] = jnp.where(
            slot[e : e + 1, :] == place, 1.0, 0.0
        ).astype(BF16)
    sent_ref[...] = lax.dot_general(
        disp_ref[...], feats, LAST, preferred_element_type=F32
    ).astype(BF16)


def weight_body(mine_ref, probs_ref, out_ref):
    mine = mine_ref[...]
    toks = mine.shape[1]
    mask = jnp.sum(mine, axis=0, keepdims=True)
    weight = jnp.sum(mine * probs_ref[...], axis=0, keepdims=True)
    rank = jnp.dot(
        jnp.broadcast_to(mask, (16, toks)).astype(BF16), before(toks), preferred_element_type=F32
    )
    place = lax.broadcasted_iota(jnp.int32, (CAP, toks), 0).astype(F32)
    hit = (rank == place) & (jnp.broadcast_to(mask, (CAP, toks)) > 0.0)
    picked = jnp.where(hit, jnp.broadcast_to(weight, (CAP, toks)), 0.0)
    out_ref[...] = jnp.broadcast_to(jnp.sum(picked, axis=1, keepdims=True), (CAP, toks))


def project_body(recv_ref, gate_ref, up_ref, down_ref, part_ref, x_ref, y_ref):
    rows = recv_ref.shape[0] // 4
    for q in range(4):
        block = recv_ref[q * rows : (q + 1) * rows, :]
        x_ref[:, q * 64 : (q + 1) * 64] = block[:, :64]
        y_ref[:, q * 64 : (q + 1) * 64] = block[:, 64:]
    x = x_ref[...]
    y = y_ref[...]
    hid = gate_ref.shape[1]
    part_ref[:, 0:hid] = jnp.dot(x, gate_ref[...], preferred_element_type=F32).astype(BF16)
    part_ref[:, hid : 2 * hid] = jnp.dot(x, up_ref[...], preferred_element_type=F32).astype(BF16)
    part_ref[:, 2 * hid : 3 * hid] = lax.dot_general(
        y, down_ref[...], LAST, preferred_element_type=F32
    ).astype(BF16)


def hidden_body(parts_ref, weight_ref, grads_ref, weighted_ref):
    peers = parts_ref.shape[0] // CAP
    hid = parts_ref.shape[1] // 3
    total = parts_ref[0:CAP, :].astype(F32)
    for s in range(1, peers):
        total = total + parts_ref[s * CAP : (s + 1) * CAP, :].astype(F32)
    gate = total[:, 0:hid]
    up = total[:, hid : 2 * hid]
    back = total[:, 2 * hid : 3 * hid]
    weight = weight_ref[:, 0:1]
    sig = jax.nn.sigmoid(gate)
    silu = gate * sig
    hidden_grad = weight * back
    hidden_weighted = (weight * silu * up).astype(BF16)
    up_grad = (hidden_grad * silu).astype(BF16)
    gate_grad = (hidden_grad * up * sig * (1.0 + gate * (1.0 - sig))).astype(BF16)
    for s in range(peers):
        rows = slice(s * CAP, (s + 1) * CAP)
        grads_ref[rows, 0:hid] = gate_grad
        grads_ref[rows, hid : 2 * hid] = up_grad
        weighted_ref[rows, :] = hidden_weighted


def slot_grad_body(grads_ref, gate_ref, up_ref, out_ref):
    hid = gate_ref.shape[1]
    slot_grad = lax.dot_general(
        grads_ref[:, 0:hid], gate_ref[...], LAST, preferred_element_type=F32
    ) + lax.dot_general(
        grads_ref[:, hid : 2 * hid], up_ref[...], LAST, preferred_element_type=F32
    )
    rows = slot_grad.shape[0]
    pairs = slot_grad.reshape(rows // 16, 2, 8, slot_grad.shape[1])
    low = pairs[:, 0].reshape(rows // 2, slot_grad.shape[1])
    high = pairs[:, 1].reshape(rows // 2, slot_grad.shape[1])
    for q in range(4):
        cols = slice(q * 64, (q + 1) * 64)
        out_ref[q * (rows // 2) : (q + 1) * (rows // 2), :] = jnp.concatenate(
            [low[:, cols], high[:, cols]], axis=1
        ).astype(BF16)


def weight_grads_body(x_ref, grads_ref, gate_ref, up_ref):
    hid = gate_ref.shape[1]
    x = x_ref[...]
    gate_ref[...] = lax.dot_general(
        x, grads_ref[:, 0:hid], FIRST, preferred_element_type=F32
    ).astype(BF16)
    up_ref[...] = lax.dot_general(
        x, grads_ref[:, hid : 2 * hid], FIRST, preferred_element_type=F32
    ).astype(BF16)


def down_grad_body(weighted_ref, y_ref, out_ref):
    out_ref[...] = lax.dot_general(
        weighted_ref[...], y_ref[...], FIRST, preferred_element_type=F32
    ).astype(BF16)


def combine_body(recv_ref, disp_ref, out_ref):
    rows = disp_ref.shape[0]
    toks = disp_ref.shape[1]
    disp = disp_ref[...].astype(F32).reshape(rows // 16, 2, 8, toks)
    low = disp[:, 0].reshape(rows // 2, toks).astype(BF16)
    high = disp[:, 1].reshape(rows // 2, toks).astype(BF16)
    recv = recv_ref[...]
    out = lax.dot_general(recv, low, FIRST, preferred_element_type=F32)[0:64, :]
    out = out + lax.dot_general(recv, high, FIRST, preferred_element_type=F32)[64:128, :]
    out_ref[...] = out.astype(BF16)


def per_device(tokens, out_grad, probs, expert_ids, w_gate, w_up, w_down):
    blocks = lax.axis_size("ep")
    experts = lax.axis_size("edp")
    toks, width = tokens.shape
    share = experts // blocks
    slots = blocks * CAP
    wide = w_gate.shape[1]
    hid = w_gate.shape[2]
    gate, up, down = w_gate[0], w_up[0], w_down[0]

    there = [
        (b * experts + j, (j // share) * experts + (j % share) * blocks + b)
        for b in range(blocks)
        for j in range(experts)
    ]
    back = [(d, s) for s, d in there]

    ids = expert_ids.T
    packed = jnp.concatenate(
        [tokens.T, out_grad.T, ids.astype(BF16), jnp.zeros((8, toks), BF16)], axis=0
    )
    packed = lax.ppermute(packed, ("ep", "edp"), there)

    mine = (ids == lax.axis_index("edp")).astype(F32)
    weight = call(weight_body, arr((CAP, toks), F32), 10**5, 10**4, mine, probs.T)

    def body(*refs):
        dispatch_body(experts, *refs)

    sent, disp = call(
        body,
        (arr((experts * CAP, 2 * width)), arr((experts * CAP, toks))),
        2 * experts * CAP * toks * 2 * width,
        6 * 10**5,
        packed,
    )
    recv = lax.all_to_all(
        sent.reshape(experts, CAP, 2 * width), "edp", split_axis=0, concat_axis=0, tiled=True
    ).reshape(experts * CAP, 2 * width)

    part, x_s, y_s = call(
        project_body,
        (arr((slots, 3 * hid)), arr((slots, wide)), arr((slots, wide))),
        6 * slots * wide * hid,
        4 * 10**6,
        recv,
        gate,
        up,
        down,
    )
    parts = lax.all_to_all(
        part.reshape(blocks, CAP, 3 * hid), "ep", split_axis=0, concat_axis=0, tiled=True
    ).reshape(slots, 3 * hid)

    grads, weighted = call(
        hidden_body,
        (arr((slots, 2 * hid)), arr((slots, hid))),
        10**6,
        3 * 10**6,
        parts,
        weight,
    )
    grads = lax.all_to_all(
        grads.reshape(blocks, CAP, 2 * hid), "ep", split_axis=0, concat_axis=0, tiled=True
    ).reshape(slots, 2 * hid)
    weighted = lax.all_to_all(
        weighted.reshape(blocks, CAP, hid), "ep", split_axis=0, concat_axis=0, tiled=True
    ).reshape(slots, hid)

    slot_grad = call(
        slot_grad_body,
        arr((4 * slots // 2, 128)),
        4 * slots * wide * hid,
        2 * 10**6,
        grads,
        gate,
        up,
    )
    returned = lax.all_to_all(
        slot_grad.reshape(experts, 8, 128), "edp", split_axis=0, concat_axis=0, tiled=True
    ).reshape(experts * 8, 128)

    grad_gate, grad_up = call(
        weight_grads_body,
        (arr((wide, hid)), arr((wide, hid))),
        4 * slots * wide * hid,
        2 * 10**6,
        x_s,
        grads,
    )
    grad_down = call(
        down_grad_body, arr((hid, wide)), 2 * slots * wide * hid, 10**6, weighted, y_s
    )
    token_grad = call(
        combine_body, arr((width, toks)), 4 * experts * 8 * 128 * toks, 4 * 10**5, returned, disp
    )
    token_grad = lax.ppermute(token_grad, ("ep", "edp"), back).T
    return (token_grad, grad_gate[None], grad_up[None], grad_down[None])


def solution(mesh):
    placed = (
        P("ep", "edp"),
        P("ep", "edp"),
        P("ep", None),
        P("ep", None),
        P("edp", "ep", None),
        P("edp", "ep", None),
        P("edp", None, "ep"),
    )
    return jax.shard_map(
        per_device,
        mesh=mesh,
        in_specs=placed,
        out_specs=(
            P("ep", "edp"),
            P("edp", "ep", None),
            P("edp", "ep", None),
            P("edp", None, "ep"),
        ),
        check_vma=False,
    )
```

```python
import jax
import jax.numpy as jnp
from jax import lax
from jax.experimental import pallas as pl
from jax.experimental.pallas import tpu as pltpu
from jax.sharding import PartitionSpec as P

CAP = 16
BF16 = jnp.bfloat16
F32 = jnp.float32
LAST = (((1,), (1,)), ((), ()))
FIRST = (((0,), (0,)), ((), ()))


def call(body, outs, flops, moved, *args):
    return pl.pallas_call(
        body,
        out_shape=outs,
        compiler_params=pltpu.CompilerParams(vmem_limit_bytes=40 * 1024 * 1024),
        cost_estimate=pl.CostEstimate(flops=flops, bytes_accessed=moved, transcendentals=0),
    )(*args)


def arr(shape, dtype=BF16):
    return jax.ShapeDtypeStruct(shape, dtype)


def before(toks):
    row = lax.broadcasted_iota(jnp.int32, (toks, toks), 0)
    col = lax.broadcasted_iota(jnp.int32, (toks, toks), 1)
    return jnp.where(row < col, 1.0, 0.0).astype(BF16)


def dispatch_body(experts, packed_ref, sent_ref, disp_ref):
    feats = packed_ref[0:128, :]
    ids = packed_ref[128:144, :].astype(F32)
    toks = ids.shape[1]
    names = lax.broadcasted_iota(jnp.int32, (experts, toks), 0).astype(F32)
    mask = jnp.zeros((experts, toks), F32)
    for k in range(8):
        mask = mask + jnp.where(ids[k : k + 1, :] == names, 1.0, 0.0)
    rank = jnp.dot(mask.astype(BF16), before(toks), preferred_element_type=F32)
    slot = jnp.where(mask > 0.0, rank, -1.0)
    place = lax.broadcasted_iota(jnp.int32, (CAP, toks), 0).astype(F32)
    for e in range(experts):
        disp_ref[e * CAP : (e + 1) * CAP, :] = jnp.where(
            slot[e : e + 1, :] == place, 1.0, 0.0
        ).astype(BF16)
    sent_ref[...] = lax.dot_general(
        disp_ref[...], feats, LAST, preferred_element_type=F32
    ).astype(BF16)


def weight_body(mine_ref, probs_ref, out_ref):
    mine = mine_ref[...]
    toks = mine.shape[1]
    mask = jnp.sum(mine, axis=0, keepdims=True)
    weight = jnp.sum(mine * probs_ref[...], axis=0, keepdims=True)
    rank = jnp.dot(
        jnp.broadcast_to(mask, (16, toks)).astype(BF16), before(toks), preferred_element_type=F32
    )
    place = lax.broadcasted_iota(jnp.int32, (CAP, toks), 0).astype(F32)
    hit = (rank == place) & (jnp.broadcast_to(mask, (CAP, toks)) > 0.0)
    picked = jnp.where(hit, jnp.broadcast_to(weight, (CAP, toks)), 0.0)
    out_ref[...] = jnp.broadcast_to(jnp.sum(picked, axis=1, keepdims=True), (CAP, toks))


def project_body(
    recv_ref, gate_hbm, up_hbm, down_hbm, part_ref, x_ref, y_ref, gate_ref, up_ref, down_ref, sems
):
    loads = [
        pltpu.make_async_copy(src, dst, sems.at[k])
        for k, (src, dst) in enumerate(
            ((gate_hbm, gate_ref), (up_hbm, up_ref), (down_hbm, down_ref))
        )
    ]
    for load in loads:
        load.start()
    rows = recv_ref.shape[0] // 4
    for q in range(4):
        block = recv_ref[q * rows : (q + 1) * rows, :]
        x_ref[:, q * 64 : (q + 1) * 64] = block[:, :64]
        y_ref[:, q * 64 : (q + 1) * 64] = block[:, 64:]
    x = x_ref[...]
    y = y_ref[...]
    hid = gate_ref.shape[1]
    loads[0].wait()
    part_ref[:, 0:hid] = jnp.dot(x, gate_ref[...], preferred_element_type=F32).astype(BF16)
    loads[1].wait()
    part_ref[:, hid : 2 * hid] = jnp.dot(x, up_ref[...], preferred_element_type=F32).astype(BF16)
    loads[2].wait()
    part_ref[:, 2 * hid : 3 * hid] = lax.dot_general(
        y, down_ref[...], LAST, preferred_element_type=F32
    ).astype(BF16)


def hidden_body(parts_ref, weight_ref, grads_ref):
    peers = parts_ref.shape[0] // CAP
    hid = parts_ref.shape[1] // 3
    total = parts_ref[0:CAP, :].astype(F32)
    for s in range(1, peers):
        total = total + parts_ref[s * CAP : (s + 1) * CAP, :].astype(F32)
    gate = total[:, 0:hid]
    up = total[:, hid : 2 * hid]
    back = total[:, 2 * hid : 3 * hid]
    weight = weight_ref[:, 0:1]
    sig = jax.nn.sigmoid(gate)
    silu = gate * sig
    hidden_grad = weight * back
    hidden_weighted = (weight * silu * up).astype(BF16)
    up_grad = (hidden_grad * silu).astype(BF16)
    gate_grad = (hidden_grad * up * sig * (1.0 + gate * (1.0 - sig))).astype(BF16)
    for s in range(peers):
        rows = slice(s * CAP, (s + 1) * CAP)
        grads_ref[rows, 0:hid] = gate_grad
        grads_ref[rows, hid : 2 * hid] = up_grad
        grads_ref[rows, 2 * hid : 3 * hid] = hidden_weighted


def slot_grad_body(grads_ref, gate_ref, up_ref, out_ref):
    hid = gate_ref.shape[1]
    slot_grad = lax.dot_general(
        grads_ref[:, 0:hid], gate_ref[...], LAST, preferred_element_type=F32
    ) + lax.dot_general(
        grads_ref[:, hid : 2 * hid], up_ref[...], LAST, preferred_element_type=F32
    )
    rows = slot_grad.shape[0]
    pairs = slot_grad.reshape(rows // 16, 2, 8, slot_grad.shape[1])
    low = pairs[:, 0].reshape(rows // 2, slot_grad.shape[1])
    high = pairs[:, 1].reshape(rows // 2, slot_grad.shape[1])
    for q in range(4):
        cols = slice(q * 64, (q + 1) * 64)
        out_ref[q * (rows // 2) : (q + 1) * (rows // 2), :] = jnp.concatenate(
            [low[:, cols], high[:, cols]], axis=1
        ).astype(BF16)


def weight_grads_body(x_ref, y_ref, grads_ref, gate_ref, up_ref, down_ref):
    hid = gate_ref.shape[1]
    x = x_ref[...]
    gate_ref[...] = lax.dot_general(
        x, grads_ref[:, 0:hid], FIRST, preferred_element_type=F32
    ).astype(BF16)
    up_ref[...] = lax.dot_general(
        x, grads_ref[:, hid : 2 * hid], FIRST, preferred_element_type=F32
    ).astype(BF16)
    down_ref[...] = lax.dot_general(
        grads_ref[:, 2 * hid : 3 * hid], y_ref[...], FIRST, preferred_element_type=F32
    ).astype(BF16)


def combine_body(recv_ref, disp_ref, out_ref):
    rows = disp_ref.shape[0]
    toks = disp_ref.shape[1]
    disp = disp_ref[...].astype(F32).reshape(rows // 16, 2, 8, toks)
    low = disp[:, 0].reshape(rows // 2, toks).astype(BF16)
    high = disp[:, 1].reshape(rows // 2, toks).astype(BF16)
    recv = recv_ref[...]
    out = lax.dot_general(recv, low, FIRST, preferred_element_type=F32)[0:64, :]
    out = out + lax.dot_general(recv, high, FIRST, preferred_element_type=F32)[64:128, :]
    out_ref[...] = out.astype(BF16)


def per_device(tokens, out_grad, probs, expert_ids, w_gate, w_up, w_down):
    blocks = lax.axis_size("ep")
    experts = lax.axis_size("edp")
    toks, width = tokens.shape
    share = experts // blocks
    slots = blocks * CAP
    wide = w_gate.shape[1]
    hid = w_gate.shape[2]
    gate, up, down = w_gate[0], w_up[0], w_down[0]

    there = [
        (b * experts + j, (j // share) * experts + (j % share) * blocks + b)
        for b in range(blocks)
        for j in range(experts)
    ]
    back = [(d, s) for s, d in there]

    ids = expert_ids.T
    packed = jnp.concatenate(
        [tokens.T, out_grad.T, ids.astype(BF16), jnp.zeros((8, toks), BF16)], axis=0
    )
    packed = lax.ppermute(packed, ("ep", "edp"), there)

    mine = (ids == lax.axis_index("edp")).astype(F32)
    weight = call(weight_body, arr((CAP, toks), F32), 10**5, 10**4, mine, probs.T)

    packed, weight = lax.optimization_barrier((packed, weight))

    def body(*refs):
        dispatch_body(experts, *refs)

    sent, disp = call(
        body,
        (arr((experts * CAP, 2 * width)), arr((experts * CAP, toks))),
        2 * experts * CAP * toks * 2 * width,
        6 * 10**5,
        packed,
    )
    recv = lax.all_to_all(
        sent.reshape(experts, CAP, 2 * width), "edp", split_axis=0, concat_axis=0, tiled=True
    ).reshape(experts * CAP, 2 * width)

    part, x_s, y_s = pl.pallas_call(
        project_body,
        out_shape=(arr((slots, 3 * hid)), arr((slots, wide)), arr((slots, wide))),
        in_specs=[pl.BlockSpec(memory_space=pltpu.VMEM)]
        + [pl.BlockSpec(memory_space=pl.ANY)] * 3,
        scratch_shapes=[
            pltpu.VMEM((wide, hid), BF16),
            pltpu.VMEM((wide, hid), BF16),
            pltpu.VMEM((hid, wide), BF16),
            pltpu.SemaphoreType.DMA((3,)),
        ],
        compiler_params=pltpu.CompilerParams(vmem_limit_bytes=40 * 1024 * 1024),
        cost_estimate=pl.CostEstimate(
            flops=6 * slots * wide * hid, bytes_accessed=4 * 10**6, transcendentals=0
        ),
    )(recv, gate, up, down)
    parts = lax.all_to_all(
        part.reshape(blocks, CAP, 3 * hid), "ep", split_axis=0, concat_axis=0, tiled=True
    ).reshape(slots, 3 * hid)

    grads = call(hidden_body, arr((slots, 3 * hid)), 10**6, 3 * 10**6, parts, weight)
    grads = lax.all_to_all(
        grads.reshape(blocks, CAP, 3 * hid), "ep", split_axis=0, concat_axis=0, tiled=True
    ).reshape(slots, 3 * hid)

    slot_grad = call(
        slot_grad_body,
        arr((4 * slots // 2, 128)),
        4 * slots * wide * hid,
        2 * 10**6,
        grads,
        gate,
        up,
    )
    returned = lax.all_to_all(
        slot_grad.reshape(experts, 8, 128), "edp", split_axis=0, concat_axis=0, tiled=True
    ).reshape(experts * 8, 128)

    token_grad = call(
        combine_body, arr((width, toks)), 4 * experts * 8 * 128 * toks, 4 * 10**5, returned, disp
    )
    grads, token_grad = lax.optimization_barrier((grads, token_grad))
    grad_gate, grad_up, grad_down = call(
        weight_grads_body,
        (arr((wide, hid)), arr((wide, hid)), arr((hid, wide))),
        6 * slots * wide * hid,
        4 * 10**6,
        x_s,
        y_s,
        grads,
    )
    token_grad = lax.ppermute(token_grad, ("ep", "edp"), back).T
    return (token_grad, grad_gate[None], grad_up[None], grad_down[None])


def solution(mesh):
    placed = (
        P("ep", "edp"),
        P("ep", "edp"),
        P("ep", None),
        P("ep", None),
        P("edp", "ep", None),
        P("edp", "ep", None),
        P("edp", None, "ep"),
    )
    return jax.shard_map(
        per_device,
        mesh=mesh,
        in_specs=placed,
        out_specs=(
            P("ep", "edp"),
            P("edp", "ep", None),
            P("edp", "ep", None),
            P("edp", None, "ep"),
        ),
        check_vma=False,
    )
```

```python
import jax
import jax.numpy as jnp
from jax import lax
from jax.experimental import pallas as pl
from jax.experimental.pallas import tpu as pltpu
from jax.sharding import PartitionSpec as P

CAP = 16
BF16 = jnp.bfloat16
F32 = jnp.float32
LAST = (((1,), (1,)), ((), ()))
FIRST = (((0,), (0,)), ((), ()))


def call(body, outs, flops, moved, *args):
    return pl.pallas_call(
        body,
        out_shape=outs,
        compiler_params=pltpu.CompilerParams(vmem_limit_bytes=40 * 1024 * 1024),
        cost_estimate=pl.CostEstimate(flops=flops, bytes_accessed=moved, transcendentals=0),
    )(*args)


def arr(shape, dtype=BF16):
    return jax.ShapeDtypeStruct(shape, dtype)


def before(toks):
    row = lax.broadcasted_iota(jnp.int32, (toks, toks), 0)
    col = lax.broadcasted_iota(jnp.int32, (toks, toks), 1)
    return jnp.where(row < col, 1.0, 0.0).astype(BF16)


def dispatch_body(experts, packed_ref, sent_ref, disp_ref):
    feats = packed_ref[0:128, :]
    ids = packed_ref[128:144, :].astype(F32)
    toks = ids.shape[1]
    names = lax.broadcasted_iota(jnp.int32, (experts, toks), 0).astype(F32)
    mask = jnp.zeros((experts, toks), F32)
    for k in range(8):
        mask = mask + jnp.where(ids[k : k + 1, :] == names, 1.0, 0.0)
    rank = jnp.dot(mask.astype(BF16), before(toks), preferred_element_type=F32)
    slot = jnp.where(mask > 0.0, rank, -1.0)
    place = lax.broadcasted_iota(jnp.int32, (CAP, toks), 0).astype(F32)
    for e in range(experts):
        disp_ref[e * CAP : (e + 1) * CAP, :] = jnp.where(
            slot[e : e + 1, :] == place, 1.0, 0.0
        ).astype(BF16)
    sent_ref[...] = lax.dot_general(
        disp_ref[...], feats, LAST, preferred_element_type=F32
    ).astype(BF16)


def weight_body(mine_ref, probs_ref, gate_ref, up_ref, down_ref, out_ref):
    mine = mine_ref[...]
    toks = mine.shape[1]
    mask = jnp.sum(mine, axis=0, keepdims=True)
    weight = jnp.sum(mine * probs_ref[...], axis=0, keepdims=True)
    rank = jnp.dot(
        jnp.broadcast_to(mask, (16, toks)).astype(BF16), before(toks), preferred_element_type=F32
    )
    place = lax.broadcasted_iota(jnp.int32, (CAP, toks), 0).astype(F32)
    hit = (rank == place) & (jnp.broadcast_to(mask, (CAP, toks)) > 0.0)
    picked = jnp.where(hit, jnp.broadcast_to(weight, (CAP, toks)), 0.0)
    out_ref[...] = jnp.broadcast_to(jnp.sum(picked, axis=1, keepdims=True), (CAP, toks))


def project_body(
    recv_ref, gate_hbm, up_hbm, down_hbm, part_ref, x_ref, y_ref, gate_ref, up_ref, down_ref, sems
):
    loads = [
        pltpu.make_async_copy(src, dst, sems.at[k])
        for k, (src, dst) in enumerate(
            ((gate_hbm, gate_ref), (up_hbm, up_ref), (down_hbm, down_ref))
        )
    ]
    for load in loads:
        load.start()
    rows = recv_ref.shape[0] // 4
    recv = recv_ref[...].reshape(rows // CAP, 4, CAP, 128)
    for q in range(4):
        block = recv[:, q].reshape(rows, 128)
        x_ref[:, q * 64 : (q + 1) * 64] = block[:, :64]
        y_ref[:, q * 64 : (q + 1) * 64] = block[:, 64:]
    x = x_ref[...]
    y = y_ref[...]
    hid = gate_ref.shape[1]
    loads[0].wait()
    part_ref[:, 0:hid] = jnp.dot(x, gate_ref[...], preferred_element_type=F32).astype(BF16)
    loads[1].wait()
    part_ref[:, hid : 2 * hid] = jnp.dot(x, up_ref[...], preferred_element_type=F32).astype(BF16)
    loads[2].wait()
    part_ref[:, 2 * hid : 3 * hid] = lax.dot_general(
        y, down_ref[...], LAST, preferred_element_type=F32
    ).astype(BF16)


def hidden_body(parts_ref, weight_ref, grads_ref):
    peers = parts_ref.shape[0] // CAP
    hid = parts_ref.shape[1] // 3
    total = parts_ref[0:CAP, :].astype(F32)
    for s in range(1, peers):
        total = total + parts_ref[s * CAP : (s + 1) * CAP, :].astype(F32)
    gate = total[:, 0:hid]
    up = total[:, hid : 2 * hid]
    back = total[:, 2 * hid : 3 * hid]
    weight = weight_ref[:, 0:1]
    sig = jax.nn.sigmoid(gate)
    silu = gate * sig
    hidden_grad = weight * back
    hidden_weighted = (weight * silu * up).astype(BF16)
    up_grad = (hidden_grad * silu).astype(BF16)
    gate_grad = (hidden_grad * up * sig * (1.0 + gate * (1.0 - sig))).astype(BF16)
    for s in range(peers):
        rows = slice(s * CAP, (s + 1) * CAP)
        grads_ref[rows, 0:hid] = gate_grad
        grads_ref[rows, hid : 2 * hid] = up_grad
        grads_ref[rows, 2 * hid : 3 * hid] = hidden_weighted


def slot_grad_body(grads_ref, gate_ref, up_ref, out_ref):
    hid = gate_ref.shape[1]
    slot_grad = lax.dot_general(
        grads_ref[:, 0:hid], gate_ref[...], LAST, preferred_element_type=F32
    ) + lax.dot_general(
        grads_ref[:, hid : 2 * hid], up_ref[...], LAST, preferred_element_type=F32
    )
    blocks = slot_grad.shape[0] // CAP
    wide = slot_grad.shape[1]
    pairs = slot_grad.reshape(blocks, 2, 8, wide)
    low, high = pairs[:, 0], pairs[:, 1]
    shares = []
    for q in range(4):
        cols = slice(q * 64, (q + 1) * 64)
        shares.append(jnp.concatenate([low[:, :, cols], high[:, :, cols]], axis=2)[:, None])
    out = jnp.concatenate(shares, axis=1).reshape(4 * 8 * blocks, 128)
    out_ref[...] = out.astype(BF16)


def weight_grads_body(x_ref, y_ref, grads_ref, gate_ref, up_ref, down_ref):
    hid = gate_ref.shape[1]
    x = x_ref[...]
    gate_ref[...] = lax.dot_general(
        x, grads_ref[:, 0:hid], FIRST, preferred_element_type=F32
    ).astype(BF16)
    up_ref[...] = lax.dot_general(
        x, grads_ref[:, hid : 2 * hid], FIRST, preferred_element_type=F32
    ).astype(BF16)
    down_ref[...] = lax.dot_general(
        grads_ref[:, 2 * hid : 3 * hid], y_ref[...], FIRST, preferred_element_type=F32
    ).astype(BF16)


def combine_body(recv_ref, disp_ref, out_ref):
    rows = disp_ref.shape[0]
    toks = disp_ref.shape[1]
    disp = disp_ref[...].astype(F32).reshape(rows // 16, 2, 8, toks)
    low = disp[:, 0].reshape(rows // 2, toks).astype(BF16)
    high = disp[:, 1].reshape(rows // 2, toks).astype(BF16)
    recv = recv_ref[...]
    out = lax.dot_general(recv, low, FIRST, preferred_element_type=F32)[0:64, :]
    out = out + lax.dot_general(recv, high, FIRST, preferred_element_type=F32)[64:128, :]
    out_ref[...] = out.astype(BF16)


def per_device(tokens, out_grad, probs, expert_ids, w_gate, w_up, w_down):
    blocks = lax.axis_size("ep")
    experts = lax.axis_size("edp")
    toks, width = tokens.shape
    share = experts // blocks
    slots = blocks * CAP
    wide = w_gate.shape[1]
    hid = w_gate.shape[2]
    gate, up, down = w_gate[0], w_up[0], w_down[0]

    there = [
        (b * experts + j, (j // share) * experts + b * share + j % share)
        for b in range(blocks)
        for j in range(experts)
    ]
    back = [(d, s) for s, d in there]

    ids = expert_ids.T
    packed = jnp.concatenate(
        [tokens.T, out_grad.T, ids.astype(BF16), jnp.zeros((8, toks), BF16)], axis=0
    )
    packed = lax.ppermute(packed, ("ep", "edp"), there)

    mine = (ids == lax.axis_index("edp")).astype(F32)
    weight = pl.pallas_call(
        weight_body,
        out_shape=arr((CAP, toks), F32),
        in_specs=[pl.BlockSpec(memory_space=pltpu.VMEM)] * 2
        + [pl.BlockSpec(memory_space=pl.ANY)] * 3,
        cost_estimate=pl.CostEstimate(flops=10**5, bytes_accessed=10**4, transcendentals=0),
    )(mine, probs.T, gate, up, down)

    packed, weight = lax.optimization_barrier((packed, weight))

    def body(*refs):
        dispatch_body(experts, *refs)

    sent, disp = call(
        body,
        (arr((experts * CAP, 2 * width)), arr((experts * CAP, toks))),
        2 * experts * CAP * toks * 2 * width,
        6 * 10**5,
        packed,
    )
    recv = lax.all_to_all(
        sent.reshape(experts, CAP, 2 * width), "edp", split_axis=0, concat_axis=0, tiled=True
    ).reshape(experts * CAP, 2 * width)

    part, x_s, y_s = pl.pallas_call(
        project_body,
        out_shape=(arr((slots, 3 * hid)), arr((slots, wide)), arr((slots, wide))),
        in_specs=[pl.BlockSpec(memory_space=pltpu.VMEM)]
        + [pl.BlockSpec(memory_space=pl.ANY)] * 3,
        scratch_shapes=[
            pltpu.VMEM((wide, hid), BF16),
            pltpu.VMEM((wide, hid), BF16),
            pltpu.VMEM((hid, wide), BF16),
            pltpu.SemaphoreType.DMA((3,)),
        ],
        compiler_params=pltpu.CompilerParams(vmem_limit_bytes=40 * 1024 * 1024),
        cost_estimate=pl.CostEstimate(
            flops=6 * slots * wide * hid, bytes_accessed=4 * 10**6, transcendentals=0
        ),
    )(recv, gate, up, down)
    parts = lax.all_to_all(
        part.reshape(blocks, CAP, 3 * hid), "ep", split_axis=0, concat_axis=0, tiled=True
    ).reshape(slots, 3 * hid)

    grads = call(hidden_body, arr((slots, 3 * hid)), 10**6, 3 * 10**6, parts, weight)
    grads = lax.all_to_all(
        grads.reshape(blocks, CAP, 3 * hid), "ep", split_axis=0, concat_axis=0, tiled=True
    ).reshape(slots, 3 * hid)

    slot_grad = call(
        slot_grad_body,
        arr((4 * slots // 2, 128)),
        4 * slots * wide * hid,
        2 * 10**6,
        grads,
        gate,
        up,
    )
    returned = lax.all_to_all(
        slot_grad.reshape(experts, 8, 128), "edp", split_axis=0, concat_axis=0, tiled=True
    ).reshape(experts * 8, 128)

    token_grad = call(
        combine_body, arr((width, toks)), 4 * experts * 8 * 128 * toks, 4 * 10**5, returned, disp
    )
    grads, token_grad = lax.optimization_barrier((grads, token_grad))
    grad_gate, grad_up, grad_down = call(
        weight_grads_body,
        (arr((wide, hid)), arr((wide, hid)), arr((hid, wide))),
        6 * slots * wide * hid,
        4 * 10**6,
        x_s,
        y_s,
        grads,
    )
    token_grad = lax.ppermute(token_grad, ("ep", "edp"), back).T
    return (token_grad, grad_gate[None], grad_up[None], grad_down[None])


def solution(mesh):
    placed = (
        P("ep", "edp"),
        P("ep", "edp"),
        P("ep", None),
        P("ep", None),
        P("edp", "ep", None),
        P("edp", "ep", None),
        P("edp", None, "ep"),
    )
    return jax.shard_map(
        per_device,
        mesh=mesh,
        in_specs=placed,
        out_specs=(
            P("ep", "edp"),
            P("edp", "ep", None),
            P("edp", "ep", None),
            P("edp", None, "ep"),
        ),
        check_vma=False,
    )
```

```python
import jax
import jax.numpy as jnp
from jax import lax
from jax.experimental import pallas as pl
from jax.experimental.pallas import tpu as pltpu
from jax.sharding import PartitionSpec as P

CAP = 16
BF16 = jnp.bfloat16
F32 = jnp.float32
LAST = (((1,), (1,)), ((), ()))
FIRST = (((0,), (0,)), ((), ()))


def call(body, outs, flops, moved, *args):
    return pl.pallas_call(
        body,
        out_shape=outs,
        compiler_params=pltpu.CompilerParams(vmem_limit_bytes=40 * 1024 * 1024),
        cost_estimate=pl.CostEstimate(flops=flops, bytes_accessed=moved, transcendentals=0),
    )(*args)


def arr(shape, dtype=BF16):
    return jax.ShapeDtypeStruct(shape, dtype)


def before(toks):
    row = lax.broadcasted_iota(jnp.int32, (toks, toks), 0)
    col = lax.broadcasted_iota(jnp.int32, (toks, toks), 1)
    return jnp.where(row < col, 1.0, 0.0).astype(BF16)


def dispatch_body(experts, packed_ref, sent_ref, disp_ref):
    feats = packed_ref[0:128, :]
    ids = packed_ref[128:144, :].astype(F32)
    toks = ids.shape[1]
    names = lax.broadcasted_iota(jnp.int32, (experts, toks), 0).astype(F32)
    mask = jnp.zeros((experts, toks), F32)
    for k in range(8):
        mask = mask + jnp.where(ids[k : k + 1, :] == names, 1.0, 0.0)
    rank = jnp.dot(mask.astype(BF16), before(toks), preferred_element_type=F32)
    slot = jnp.where(mask > 0.0, rank, -1.0)
    place = lax.broadcasted_iota(jnp.int32, (CAP, toks), 0).astype(F32)
    for e in range(experts):
        disp_ref[e * CAP : (e + 1) * CAP, :] = jnp.where(
            slot[e : e + 1, :] == place, 1.0, 0.0
        ).astype(BF16)
    sent_ref[...] = lax.dot_general(
        disp_ref[...], feats, LAST, preferred_element_type=F32
    ).astype(BF16)


def weight_body(mine_ref, probs_ref, gate_ref, up_ref, down_ref, out_ref):
    mine = mine_ref[...]
    toks = mine.shape[1]
    mask = jnp.sum(mine, axis=0, keepdims=True)
    weight = jnp.sum(mine * probs_ref[...], axis=0, keepdims=True)
    rank = jnp.dot(
        jnp.broadcast_to(mask, (16, toks)).astype(BF16), before(toks), preferred_element_type=F32
    )
    place = lax.broadcasted_iota(jnp.int32, (CAP, toks), 0).astype(F32)
    hit = (rank == place) & (jnp.broadcast_to(mask, (CAP, toks)) > 0.0)
    picked = jnp.where(hit, jnp.broadcast_to(weight, (CAP, toks)), 0.0)
    out_ref[...] = jnp.broadcast_to(jnp.sum(picked, axis=1, keepdims=True), (CAP, toks))


def project_body(
    recv_ref, gate_hbm, up_hbm, down_hbm, part_ref, x_ref, y_ref, gate_ref, up_ref, down_ref, sems
):
    loads = [
        pltpu.make_async_copy(src, dst, sems.at[k])
        for k, (src, dst) in enumerate(
            ((gate_hbm, gate_ref), (up_hbm, up_ref), (down_hbm, down_ref))
        )
    ]
    for load in loads:
        load.start()
    rows = recv_ref.shape[0] // 4
    recv = recv_ref[...].reshape(rows // CAP, 4, CAP, 128)
    for q in range(4):
        block = recv[:, q].reshape(rows, 128)
        x_ref[:, q * 64 : (q + 1) * 64] = block[:, :64]
        y_ref[:, q * 64 : (q + 1) * 64] = block[:, 64:]
    x = x_ref[...]
    y = y_ref[...]
    hid = gate_ref.shape[1]
    loads[0].wait()
    part_ref[:, 0:hid] = jnp.dot(x, gate_ref[...], preferred_element_type=F32).astype(BF16)
    loads[1].wait()
    part_ref[:, hid : 2 * hid] = jnp.dot(x, up_ref[...], preferred_element_type=F32).astype(BF16)
    loads[2].wait()
    part_ref[:, 2 * hid : 3 * hid] = lax.dot_general(
        y, down_ref[...], LAST, preferred_element_type=F32
    ).astype(BF16)


def hidden_body(parts_ref, weight_ref, grads_ref):
    peers = parts_ref.shape[0] // CAP
    hid = parts_ref.shape[1] // 3
    total = parts_ref[0:CAP, :].astype(F32)
    for s in range(1, peers):
        total = total + parts_ref[s * CAP : (s + 1) * CAP, :].astype(F32)
    gate = total[:, 0:hid]
    up = total[:, hid : 2 * hid]
    back = total[:, 2 * hid : 3 * hid]
    weight = weight_ref[:, 0:1]
    sig = jax.nn.sigmoid(gate)
    silu = gate * sig
    hidden_grad = weight * back
    hidden_weighted = (weight * silu * up).astype(BF16)
    up_grad = (hidden_grad * silu).astype(BF16)
    gate_grad = (hidden_grad * up * sig * (1.0 + gate * (1.0 - sig))).astype(BF16)
    grads_ref[:, 0:hid] = gate_grad
    grads_ref[:, hid : 2 * hid] = up_grad
    grads_ref[:, 2 * hid : 3 * hid] = hidden_weighted


def slot_grad_body(steps, place_ref, *refs):
    pieces, (gate_ref, up_ref, out_ref, grads_ref) = refs[:-4], refs[-4:]
    hid = gate_ref.shape[1]
    ring = len(steps)
    spot = lax.div(place_ref[0], 4)
    side = lax.rem(lax.div(place_ref[0], 2), 2)
    way = 1 - 2 * lax.rem(place_ref[0], 2)
    for step, piece_ref in zip(steps, pieces, strict=True):
        pair = 2 * CAP * lax.rem(spot + step * way + ring, ring)
        for half, z in ((0, side), (1, 1 - side)):
            row = pl.multiple_of(pair + CAP * z, CAP)
            grads_ref[pl.ds(row, CAP), :] = piece_ref[half * CAP : (half + 1) * CAP, :]
    slot_grad = lax.dot_general(
        grads_ref[:, 0:hid], gate_ref[...], LAST, preferred_element_type=F32
    ) + lax.dot_general(
        grads_ref[:, hid : 2 * hid], up_ref[...], LAST, preferred_element_type=F32
    )
    blocks = slot_grad.shape[0] // CAP
    wide = slot_grad.shape[1]
    pairs = slot_grad.reshape(blocks, 2, 8, wide)
    low, high = pairs[:, 0], pairs[:, 1]
    shares = []
    for q in range(4):
        cols = slice(q * 64, (q + 1) * 64)
        shares.append(jnp.concatenate([low[:, :, cols], high[:, :, cols]], axis=2)[:, None])
    out = jnp.concatenate(shares, axis=1).reshape(4 * 8 * blocks, 128)
    out_ref[...] = out.astype(BF16)


def weight_grads_body(x_ref, y_ref, grads_ref, gate_ref, up_ref, down_ref):
    hid = gate_ref.shape[1]
    x = x_ref[...]
    gate_ref[...] = lax.dot_general(
        x, grads_ref[:, 0:hid], FIRST, preferred_element_type=F32
    ).astype(BF16)
    up_ref[...] = lax.dot_general(
        x, grads_ref[:, hid : 2 * hid], FIRST, preferred_element_type=F32
    ).astype(BF16)
    down_ref[...] = lax.dot_general(
        grads_ref[:, 2 * hid : 3 * hid], y_ref[...], FIRST, preferred_element_type=F32
    ).astype(BF16)


def combine_body(recv_ref, disp_ref, out_ref):
    rows = disp_ref.shape[0]
    toks = disp_ref.shape[1]
    disp = disp_ref[...].astype(F32).reshape(rows // 16, 2, 8, toks)
    low = disp[:, 0].reshape(rows // 2, toks).astype(BF16)
    high = disp[:, 1].reshape(rows // 2, toks).astype(BF16)
    recv = recv_ref[...]
    out = lax.dot_general(recv, low, FIRST, preferred_element_type=F32)[0:64, :]
    out = out + lax.dot_general(recv, high, FIRST, preferred_element_type=F32)[64:128, :]
    out_ref[...] = out.astype(BF16)


def per_device(tokens, out_grad, probs, expert_ids, w_gate, w_up, w_down):
    blocks = lax.axis_size("ep")
    experts = lax.axis_size("edp")
    toks, width = tokens.shape
    share = experts // blocks
    slots = blocks * CAP
    wide = w_gate.shape[1]
    hid = w_gate.shape[2]
    gate, up, down = w_gate[0], w_up[0], w_down[0]

    there = [
        (b * experts + j, (j // share) * experts + b * share + j % share)
        for b in range(blocks)
        for j in range(experts)
    ]
    back = [(d, s) for s, d in there]

    ids = expert_ids.T
    packed = jnp.concatenate(
        [tokens.T, out_grad.T, ids.astype(BF16), jnp.zeros((8, toks), BF16)], axis=0
    )
    packed = lax.ppermute(packed, ("ep", "edp"), there)

    mine = (ids == lax.axis_index("edp")).astype(F32)
    weight = pl.pallas_call(
        weight_body,
        out_shape=arr((CAP, toks), F32),
        in_specs=[pl.BlockSpec(memory_space=pltpu.VMEM)] * 2
        + [pl.BlockSpec(memory_space=pl.ANY)] * 3,
        cost_estimate=pl.CostEstimate(flops=10**5, bytes_accessed=10**4, transcendentals=0),
    )(mine, probs.T, gate, up, down)

    packed, weight = lax.optimization_barrier((packed, weight))

    def body(*refs):
        dispatch_body(experts, *refs)

    sent, disp = call(
        body,
        (arr((experts * CAP, 2 * width)), arr((experts * CAP, toks))),
        2 * experts * CAP * toks * 2 * width,
        6 * 10**5,
        packed,
    )
    recv = lax.all_to_all(
        sent.reshape(experts, CAP, 2 * width), "edp", split_axis=0, concat_axis=0, tiled=True
    ).reshape(experts * CAP, 2 * width)

    part, x_s, y_s = pl.pallas_call(
        project_body,
        out_shape=(arr((slots, 3 * hid)), arr((slots, wide)), arr((slots, wide))),
        in_specs=[pl.BlockSpec(memory_space=pltpu.VMEM)]
        + [pl.BlockSpec(memory_space=pl.ANY)] * 3,
        scratch_shapes=[
            pltpu.VMEM((wide, hid), BF16),
            pltpu.VMEM((wide, hid), BF16),
            pltpu.VMEM((hid, wide), BF16),
            pltpu.SemaphoreType.DMA((3,)),
        ],
        compiler_params=pltpu.CompilerParams(vmem_limit_bytes=40 * 1024 * 1024),
        cost_estimate=pl.CostEstimate(
            flops=6 * slots * wide * hid, bytes_accessed=4 * 10**6, transcendentals=0
        ),
    )(recv, gate, up, down)
    parts = lax.all_to_all(
        part.reshape(blocks, CAP, 3 * hid), "ep", split_axis=0, concat_axis=0, tiled=True
    ).reshape(slots, 3 * hid)

    mine = call(hidden_body, arr((CAP, 3 * hid)), 10**6, 2 * 10**6, parts, weight)

    ring = blocks // 2

    def shifted(step):
        return [
            (
                b * experts + e,
                ((b // 2 + (step if e % 2 == 0 else -step)) % ring * 2 + b % 2) * experts + e,
            )
            for b in range(blocks)
            for e in range(experts)
        ]

    other = lax.ppermute(mine, "ep", [(b, b ^ 1) for b in range(blocks)])
    right = left = jnp.concatenate([mine, other], axis=0)
    steps, pieces = [0], [right]
    for k in range(1, ring // 2 + 1):
        right = lax.ppermute(right, ("ep", "edp"), shifted(1))
        steps.append(-k)
        pieces.append(right)
        if k < ring - k:
            left = lax.ppermute(left, ("ep", "edp"), shifted(-1))
            steps.append(k)
            pieces.append(left)

    def slot_body(*refs):
        slot_grad_body(steps, *refs)

    code = lax.axis_index("ep") * 2 + lax.rem(lax.axis_index("edp"), 2)
    rank = jnp.full((1,), code, jnp.int32)
    slot_grad, grads = pl.pallas_call(
        slot_body,
        out_shape=(arr((4 * slots // 2, 128)), arr((slots, 3 * hid))),
        in_specs=[pl.BlockSpec(memory_space=pltpu.SMEM)]
        + [pl.BlockSpec(memory_space=pltpu.VMEM)] * (ring + 2),
        compiler_params=pltpu.CompilerParams(vmem_limit_bytes=40 * 1024 * 1024),
        cost_estimate=pl.CostEstimate(
            flops=4 * slots * wide * hid, bytes_accessed=5 * 10**6, transcendentals=0
        ),
    )(rank, *pieces, gate, up)
    returned = lax.all_to_all(
        slot_grad.reshape(experts, 8, 128), "edp", split_axis=0, concat_axis=0, tiled=True
    ).reshape(experts * 8, 128)

    token_grad = call(
        combine_body, arr((width, toks)), 4 * experts * 8 * 128 * toks, 4 * 10**5, returned, disp
    )
    grads, token_grad = lax.optimization_barrier((grads, token_grad))
    grad_gate, grad_up, grad_down = call(
        weight_grads_body,
        (arr((wide, hid)), arr((wide, hid)), arr((hid, wide))),
        6 * slots * wide * hid,
        4 * 10**6,
        x_s,
        y_s,
        grads,
    )
    token_grad = lax.ppermute(token_grad, ("ep", "edp"), back).T
    return (token_grad, grad_gate[None], grad_up[None], grad_down[None])


def solution(mesh):
    placed = (
        P("ep", "edp"),
        P("ep", "edp"),
        P("ep", None),
        P("ep", None),
        P("edp", "ep", None),
        P("edp", "ep", None),
        P("edp", None, "ep"),
    )
    return jax.shard_map(
        per_device,
        mesh=mesh,
        in_specs=placed,
        out_specs=(
            P("ep", "edp"),
            P("edp", "ep", None),
            P("edp", "ep", None),
            P("edp", None, "ep"),
        ),
        check_vma=False,
    )
```

```python
import jax
import jax.numpy as jnp
from jax import lax
from jax.experimental import pallas as pl
from jax.experimental.pallas import tpu as pltpu
from jax.sharding import PartitionSpec as P

CAP = 16
BF16 = jnp.bfloat16
F32 = jnp.float32
LAST = (((1,), (1,)), ((), ()))
FIRST = (((0,), (0,)), ((), ()))


def call(body, outs, flops, moved, *args):
    return pl.pallas_call(
        body,
        out_shape=outs,
        compiler_params=pltpu.CompilerParams(vmem_limit_bytes=40 * 1024 * 1024),
        cost_estimate=pl.CostEstimate(flops=flops, bytes_accessed=moved, transcendentals=0),
    )(*args)


def arr(shape, dtype=BF16):
    return jax.ShapeDtypeStruct(shape, dtype)


def before(toks):
    row = lax.broadcasted_iota(jnp.int32, (toks, toks), 0)
    col = lax.broadcasted_iota(jnp.int32, (toks, toks), 1)
    return jnp.where(row < col, 1.0, 0.0).astype(BF16)


def dispatch_body(experts, packed_ref, sent_ref, disp_ref):
    feats = packed_ref[0:128, :]
    ids = packed_ref[128:144, :].astype(F32)
    toks = ids.shape[1]
    names = lax.broadcasted_iota(jnp.int32, (experts, toks), 0).astype(F32)
    mask = jnp.zeros((experts, toks), F32)
    for k in range(8):
        mask = mask + jnp.where(ids[k : k + 1, :] == names, 1.0, 0.0)
    rank = jnp.dot(mask.astype(BF16), before(toks), preferred_element_type=F32)
    slot = jnp.where(mask > 0.0, rank, -1.0)
    place = lax.broadcasted_iota(jnp.int32, (CAP, toks), 0).astype(F32)
    for e in range(experts):
        disp_ref[e * CAP : (e + 1) * CAP, :] = jnp.where(
            slot[e : e + 1, :] == place, 1.0, 0.0
        ).astype(BF16)
    sent_ref[...] = lax.dot_general(
        disp_ref[...], feats, LAST, preferred_element_type=F32
    ).astype(BF16)


def weight_body(mine_ref, probs_ref, gate_ref, up_ref, down_ref, out_ref):
    mine = mine_ref[...]
    toks = mine.shape[1]
    mask = jnp.sum(mine, axis=0, keepdims=True)
    weight = jnp.sum(mine * probs_ref[...], axis=0, keepdims=True)
    rank = jnp.dot(
        jnp.broadcast_to(mask, (16, toks)).astype(BF16), before(toks), preferred_element_type=F32
    )
    place = lax.broadcasted_iota(jnp.int32, (CAP, toks), 0).astype(F32)
    hit = (rank == place) & (jnp.broadcast_to(mask, (CAP, toks)) > 0.0)
    picked = jnp.where(hit, jnp.broadcast_to(weight, (CAP, toks)), 0.0)
    out_ref[...] = jnp.broadcast_to(jnp.sum(picked, axis=1, keepdims=True), (CAP, toks))


def project_body(
    recv_ref, gate_hbm, up_hbm, down_hbm, part_ref, x_ref, y_ref, gate_ref, up_ref, down_ref, sems
):
    loads = [
        pltpu.make_async_copy(src, dst, sems.at[k])
        for k, (src, dst) in enumerate(
            ((gate_hbm, gate_ref), (up_hbm, up_ref), (down_hbm, down_ref))
        )
    ]
    for load in loads:
        load.start()
    rows = recv_ref.shape[0] // 4
    recv = recv_ref[...].reshape(rows // CAP, 4, CAP, 128)
    for q in range(4):
        block = recv[:, q].reshape(rows, 128)
        x_ref[:, q * 64 : (q + 1) * 64] = block[:, :64]
        y_ref[:, q * 64 : (q + 1) * 64] = block[:, 64:]
    x = x_ref[...]
    y = y_ref[...]
    hid = gate_ref.shape[1]
    loads[0].wait()
    part_ref[:, 0:hid] = jnp.dot(x, gate_ref[...], preferred_element_type=F32).astype(BF16)
    loads[1].wait()
    part_ref[:, hid : 2 * hid] = jnp.dot(x, up_ref[...], preferred_element_type=F32).astype(BF16)
    loads[2].wait()
    part_ref[:, 2 * hid : 3 * hid] = lax.dot_general(
        y, down_ref[...], LAST, preferred_element_type=F32
    ).astype(BF16)


def hidden_body(parts_ref, weight_ref, grads_ref):
    peers = parts_ref.shape[0] // CAP
    hid = parts_ref.shape[1] // 3
    total = parts_ref[0:CAP, :].astype(F32)
    for s in range(1, peers):
        total = total + parts_ref[s * CAP : (s + 1) * CAP, :].astype(F32)
    gate = total[:, 0:hid]
    up = total[:, hid : 2 * hid]
    back = total[:, 2 * hid : 3 * hid]
    weight = weight_ref[:, 0:1]
    sig = jax.nn.sigmoid(gate)
    silu = gate * sig
    hidden_grad = weight * back
    hidden_weighted = (weight * silu * up).astype(BF16)
    up_grad = (hidden_grad * silu).astype(BF16)
    gate_grad = (hidden_grad * up * sig * (1.0 + gate * (1.0 - sig))).astype(BF16)
    grads_ref[:, 0:hid] = gate_grad
    grads_ref[:, hid : 2 * hid] = up_grad
    grads_ref[:, 2 * hid : 3 * hid] = hidden_weighted


def slot_grad_body(steps, place_ref, *refs):
    pieces, (gate_ref, up_ref, out_ref, grads_ref) = refs[:-4], refs[-4:]
    hid = gate_ref.shape[1]
    ring = len(steps)
    spot = lax.div(place_ref[0], 4)
    side = lax.rem(lax.div(place_ref[0], 2), 2)
    way = 1 - 2 * lax.rem(place_ref[0], 2)
    for step, piece_ref in zip(steps, pieces, strict=True):
        pair = 2 * CAP * lax.rem(spot + step * way + ring, ring)
        for half, z in ((0, side), (1, 1 - side)):
            row = pl.multiple_of(pair + CAP * z, CAP)
            grads_ref[pl.ds(row, CAP), :] = piece_ref[half * CAP : (half + 1) * CAP, :]
    slot_grad = lax.dot_general(
        grads_ref[:, 0:hid], gate_ref[...], LAST, preferred_element_type=F32
    ) + lax.dot_general(
        grads_ref[:, hid : 2 * hid], up_ref[...], LAST, preferred_element_type=F32
    )
    blocks = slot_grad.shape[0] // CAP
    wide = slot_grad.shape[1]
    pairs = slot_grad.reshape(blocks, 2, 8, wide)
    low, high = pairs[:, 0], pairs[:, 1]
    shares = []
    for q in range(4):
        cols = slice(q * 64, (q + 1) * 64)
        shares.append(jnp.concatenate([low[:, :, cols], high[:, :, cols]], axis=2)[:, None])
    out = jnp.concatenate(shares, axis=1).reshape(4 * 8 * blocks, 128)
    out_ref[...] = out.astype(BF16)


def weight_grads_body(x_ref, y_ref, grads_ref, gate_ref, up_ref, down_ref):
    hid = gate_ref.shape[1]
    x = x_ref[...]
    gate_ref[...] = lax.dot_general(
        x, grads_ref[:, 0:hid], FIRST, preferred_element_type=F32
    ).astype(BF16)
    up_ref[...] = lax.dot_general(
        x, grads_ref[:, hid : 2 * hid], FIRST, preferred_element_type=F32
    ).astype(BF16)
    down_ref[...] = lax.dot_general(
        grads_ref[:, 2 * hid : 3 * hid], y_ref[...], FIRST, preferred_element_type=F32
    ).astype(BF16)


def combine_body(recv_ref, disp_ref, out_ref):
    rows = disp_ref.shape[0]
    toks = disp_ref.shape[1]
    disp = disp_ref[...].astype(F32).reshape(rows // 16, 2, 8, toks)
    low = disp[:, 0].reshape(rows // 2, toks).astype(BF16)
    high = disp[:, 1].reshape(rows // 2, toks).astype(BF16)
    recv = recv_ref[...]
    out = lax.dot_general(recv, low, FIRST, preferred_element_type=F32)[0:64, :]
    out = out + lax.dot_general(recv, high, FIRST, preferred_element_type=F32)[64:128, :]
    out_ref[...] = out.astype(BF16)


def per_device(tokens, out_grad, probs, expert_ids, w_gate, w_up, w_down):
    blocks = lax.axis_size("ep")
    experts = lax.axis_size("edp")
    toks, width = tokens.shape
    share = experts // blocks
    slots = blocks * CAP
    wide = w_gate.shape[1]
    hid = w_gate.shape[2]
    gate, up, down = w_gate[0], w_up[0], w_down[0]

    there = [
        (b * experts + j, (j // share) * experts + b * share + j % share)
        for b in range(blocks)
        for j in range(experts)
    ]
    back = [(d, s) for s, d in there]

    ids = expert_ids.T
    packed = jnp.concatenate(
        [tokens.T, out_grad.T, ids.astype(BF16), jnp.zeros((8, toks), BF16)], axis=0
    )
    packed = lax.ppermute(packed, ("ep", "edp"), there)

    mine = (ids == lax.axis_index("edp")).astype(F32)
    weight = pl.pallas_call(
        weight_body,
        out_shape=arr((CAP, toks), F32),
        in_specs=[pl.BlockSpec(memory_space=pltpu.VMEM)] * 2
        + [pl.BlockSpec(memory_space=pl.ANY)] * 3,
        cost_estimate=pl.CostEstimate(flops=10**5, bytes_accessed=10**4, transcendentals=0),
    )(mine, probs.T, gate, up, down)

    packed, weight = lax.optimization_barrier((packed, weight))

    def body(*refs):
        dispatch_body(experts, *refs)

    sent, disp = call(
        body,
        (arr((experts * CAP, 2 * width)), arr((experts * CAP, toks))),
        2 * experts * CAP * toks * 2 * width,
        6 * 10**5,
        packed,
    )
    recv = lax.all_to_all(
        sent.reshape(experts, CAP, 2 * width), "edp", split_axis=0, concat_axis=0, tiled=True
    ).reshape(experts * CAP, 2 * width)

    part, x_s, y_s = pl.pallas_call(
        project_body,
        out_shape=(arr((slots, 3 * hid)), arr((slots, wide)), arr((slots, wide))),
        in_specs=[pl.BlockSpec(memory_space=pltpu.VMEM)]
        + [pl.BlockSpec(memory_space=pl.ANY)] * 3,
        scratch_shapes=[
            pltpu.VMEM((wide, hid), BF16),
            pltpu.VMEM((wide, hid), BF16),
            pltpu.VMEM((hid, wide), BF16),
            pltpu.SemaphoreType.DMA((3,)),
        ],
        compiler_params=pltpu.CompilerParams(vmem_limit_bytes=40 * 1024 * 1024),
        cost_estimate=pl.CostEstimate(
            flops=6 * slots * wide * hid, bytes_accessed=4 * 10**6, transcendentals=0
        ),
    )(recv, gate, up, down)
    parts = lax.all_to_all(
        part.reshape(blocks, CAP, 3 * hid), "ep", split_axis=0, concat_axis=0, tiled=True
    ).reshape(slots, 3 * hid)

    mine = call(hidden_body, arr((CAP, 3 * hid)), 10**6, 2 * 10**6, parts, weight)

    ring = blocks // 2

    def shifted(step):
        return [
            (
                b * experts + e,
                ((b // 2 + (step if e % 2 == 0 else -step)) % ring * 2 + b % 2) * experts + e,
            )
            for b in range(blocks)
            for e in range(experts)
        ]

    other = lax.ppermute(mine, "ep", [(b, b ^ 1) for b in range(blocks)])
    pair = jnp.concatenate([mine, other], axis=0)

    def passed(piece, step):
        return lax.ppermute(piece, ("ep", "edp"), shifted(step))

    right_two, left_two = passed(pair, 2), passed(pair, -2)
    right_one, left_one = passed(pair, 1), passed(pair, -1)
    right_three, left_three = passed(right_two, 1), passed(left_two, -1)
    steps = [0, -2, 2, -1, 1, -3, 3, -4]
    pieces = [pair, right_two, left_two, right_one, left_one, right_three, left_three]
    pieces.append(passed(right_two, 2))

    def slot_body(*refs):
        slot_grad_body(steps, *refs)

    code = lax.axis_index("ep") * 2 + lax.rem(lax.axis_index("edp"), 2)
    rank = jnp.full((1,), code, jnp.int32)
    slot_grad, grads = pl.pallas_call(
        slot_body,
        out_shape=(arr((4 * slots // 2, 128)), arr((slots, 3 * hid))),
        in_specs=[pl.BlockSpec(memory_space=pltpu.SMEM)]
        + [pl.BlockSpec(memory_space=pltpu.VMEM)] * (ring + 2),
        compiler_params=pltpu.CompilerParams(vmem_limit_bytes=40 * 1024 * 1024),
        cost_estimate=pl.CostEstimate(
            flops=4 * slots * wide * hid, bytes_accessed=5 * 10**6, transcendentals=0
        ),
    )(rank, *pieces, gate, up)
    returned = lax.all_to_all(
        slot_grad.reshape(experts, 8, 128), "edp", split_axis=0, concat_axis=0, tiled=True
    ).reshape(experts * 8, 128)

    token_grad = call(
        combine_body, arr((width, toks)), 4 * experts * 8 * 128 * toks, 4 * 10**5, returned, disp
    )
    grads, token_grad = lax.optimization_barrier((grads, token_grad))
    grad_gate, grad_up, grad_down = call(
        weight_grads_body,
        (arr((wide, hid)), arr((wide, hid)), arr((hid, wide))),
        6 * slots * wide * hid,
        4 * 10**6,
        x_s,
        y_s,
        grads,
    )
    token_grad = lax.ppermute(token_grad, ("ep", "edp"), back).T
    return (token_grad, grad_gate[None], grad_up[None], grad_down[None])


def solution(mesh):
    placed = (
        P("ep", "edp"),
        P("ep", "edp"),
        P("ep", None),
        P("ep", None),
        P("edp", "ep", None),
        P("edp", "ep", None),
        P("edp", None, "ep"),
    )
    return jax.shard_map(
        per_device,
        mesh=mesh,
        in_specs=placed,
        out_specs=(
            P("ep", "edp"),
            P("edp", "ep", None),
            P("edp", "ep", None),
            P("edp", None, "ep"),
        ),
        check_vma=False,
    )
```

```python
import jax
import jax.numpy as jnp
from jax import lax
from jax.experimental import pallas as pl
from jax.experimental.pallas import tpu as pltpu
from jax.sharding import PartitionSpec as P

CAP = 16
BF16 = jnp.bfloat16
F32 = jnp.float32
LAST = (((1,), (1,)), ((), ()))
FIRST = (((0,), (0,)), ((), ()))


def call(body, outs, flops, moved, *args):
    return pl.pallas_call(
        body,
        out_shape=outs,
        compiler_params=pltpu.CompilerParams(vmem_limit_bytes=40 * 1024 * 1024),
        cost_estimate=pl.CostEstimate(flops=flops, bytes_accessed=moved, transcendentals=0),
    )(*args)


def arr(shape, dtype=BF16):
    return jax.ShapeDtypeStruct(shape, dtype)


def before(toks):
    row = lax.broadcasted_iota(jnp.int32, (toks, toks), 0)
    col = lax.broadcasted_iota(jnp.int32, (toks, toks), 1)
    return jnp.where(row < col, 1.0, 0.0).astype(BF16)


def dispatch_body(experts, packed_ref, sent_ref, disp_ref):
    feats = packed_ref[0:128, :]
    ids = packed_ref[128:144, :].astype(F32)
    toks = ids.shape[1]
    names = lax.broadcasted_iota(jnp.int32, (experts, toks), 0).astype(F32)
    mask = jnp.zeros((experts, toks), F32)
    for k in range(8):
        mask = mask + jnp.where(ids[k : k + 1, :] == names, 1.0, 0.0)
    rank = jnp.dot(mask.astype(BF16), before(toks), preferred_element_type=F32)
    slot = jnp.where(mask > 0.0, rank, -1.0)
    place = lax.broadcasted_iota(jnp.int32, (CAP, toks), 0).astype(F32)
    for e in range(experts):
        disp_ref[e * CAP : (e + 1) * CAP, :] = jnp.where(
            slot[e : e + 1, :] == place, 1.0, 0.0
        ).astype(BF16)
    sent_ref[...] = lax.dot_general(
        disp_ref[...], feats, LAST, preferred_element_type=F32
    ).astype(BF16)


def weight_body(experts, place_ref, ids_ref, probs_ref, gate_ref, up_ref, down_ref, out_ref):
    mine = jnp.where(ids_ref[...] == lax.rem(place_ref[0], experts), 1.0, 0.0)
    toks = mine.shape[1]
    mask = jnp.sum(mine, axis=0, keepdims=True)
    weight = jnp.sum(mine * probs_ref[...], axis=0, keepdims=True)
    rank = jnp.dot(
        jnp.broadcast_to(mask, (16, toks)).astype(BF16), before(toks), preferred_element_type=F32
    )
    place = lax.broadcasted_iota(jnp.int32, (CAP, toks), 0).astype(F32)
    hit = (rank == place) & (jnp.broadcast_to(mask, (CAP, toks)) > 0.0)
    picked = jnp.where(hit, jnp.broadcast_to(weight, (CAP, toks)), 0.0)
    out_ref[...] = jnp.broadcast_to(jnp.sum(picked, axis=1, keepdims=True), (CAP, toks))


def project_body(
    recv_ref, gate_hbm, up_hbm, down_hbm, part_ref, x_ref, y_ref, gate_ref, up_ref, down_ref, sems
):
    loads = [
        pltpu.make_async_copy(src, dst, sems.at[k])
        for k, (src, dst) in enumerate(
            ((gate_hbm, gate_ref), (up_hbm, up_ref), (down_hbm, down_ref))
        )
    ]
    for load in loads:
        load.start()
    rows = recv_ref.shape[0] // 4
    recv = recv_ref[...].reshape(rows // CAP, 4, CAP, 128)
    for q in range(4):
        block = recv[:, q].reshape(rows, 128)
        x_ref[:, q * 64 : (q + 1) * 64] = block[:, :64]
        y_ref[:, q * 64 : (q + 1) * 64] = block[:, 64:]
    x = x_ref[...]
    y = y_ref[...]
    hid = gate_ref.shape[1]
    loads[0].wait()
    part_ref[:, 0:hid] = jnp.dot(x, gate_ref[...], preferred_element_type=F32).astype(BF16)
    loads[1].wait()
    part_ref[:, hid : 2 * hid] = jnp.dot(x, up_ref[...], preferred_element_type=F32).astype(BF16)
    loads[2].wait()
    part_ref[:, 2 * hid : 3 * hid] = lax.dot_general(
        y, down_ref[...], LAST, preferred_element_type=F32
    ).astype(BF16)


def hidden_body(parts_ref, weight_ref, grads_ref):
    peers = parts_ref.shape[0] // CAP
    hid = parts_ref.shape[1] // 3
    total = parts_ref[0:CAP, :].astype(F32)
    for s in range(1, peers):
        total = total + parts_ref[s * CAP : (s + 1) * CAP, :].astype(F32)
    gate = total[:, 0:hid]
    up = total[:, hid : 2 * hid]
    back = total[:, 2 * hid : 3 * hid]
    weight = weight_ref[:, 0:1]
    sig = jax.nn.sigmoid(gate)
    silu = gate * sig
    hidden_grad = weight * back
    hidden_weighted = (weight * silu * up).astype(BF16)
    up_grad = (hidden_grad * silu).astype(BF16)
    gate_grad = (hidden_grad * up * sig * (1.0 + gate * (1.0 - sig))).astype(BF16)
    grads_ref[:, 0:hid] = gate_grad
    grads_ref[:, hid : 2 * hid] = up_grad
    grads_ref[:, 2 * hid : 3 * hid] = hidden_weighted


def slot_grad_body(experts, steps, place_ref, *refs):
    pieces, (gate_ref, up_ref, out_ref, grads_ref) = refs[:-4], refs[-4:]
    hid = gate_ref.shape[1]
    ring = sum(len(held) for held in steps)
    spot = lax.div(place_ref[0], 2 * experts)
    side = lax.rem(lax.div(place_ref[0], experts), 2)
    way = 1 - 2 * lax.rem(place_ref[0], 2)
    for held, piece_ref in zip(steps, pieces, strict=True):
        for at, step in enumerate(held):
            pair = 2 * CAP * lax.rem(spot + step * way + ring, ring)
            for half, z in ((0, side), (1, 1 - side)):
                row = pl.multiple_of(pair + CAP * z, CAP)
                low = (2 * at + half) * CAP
                grads_ref[pl.ds(row, CAP), :] = piece_ref[low : low + CAP, :]
    slot_grad = lax.dot_general(
        grads_ref[:, 0:hid], gate_ref[...], LAST, preferred_element_type=F32
    ) + lax.dot_general(
        grads_ref[:, hid : 2 * hid], up_ref[...], LAST, preferred_element_type=F32
    )
    blocks = slot_grad.shape[0] // CAP
    wide = slot_grad.shape[1]
    pairs = slot_grad.reshape(blocks, 2, 8, wide)
    low, high = pairs[:, 0], pairs[:, 1]
    shares = []
    for q in range(4):
        cols = slice(q * 64, (q + 1) * 64)
        shares.append(jnp.concatenate([low[:, :, cols], high[:, :, cols]], axis=2)[:, None])
    out = jnp.concatenate(shares, axis=1).reshape(4 * 8 * blocks, 128)
    out_ref[...] = out.astype(BF16)


def weight_grads_body(x_ref, y_ref, grads_ref, gate_ref, up_ref, down_ref):
    hid = gate_ref.shape[1]
    x = x_ref[...]
    gate_ref[...] = lax.dot_general(
        x, grads_ref[:, 0:hid], FIRST, preferred_element_type=F32
    ).astype(BF16)
    up_ref[...] = lax.dot_general(
        x, grads_ref[:, hid : 2 * hid], FIRST, preferred_element_type=F32
    ).astype(BF16)
    down_ref[...] = lax.dot_general(
        grads_ref[:, 2 * hid : 3 * hid], y_ref[...], FIRST, preferred_element_type=F32
    ).astype(BF16)


def combine_body(recv_ref, disp_ref, out_ref):
    rows = disp_ref.shape[0]
    toks = disp_ref.shape[1]
    disp = disp_ref[...].astype(F32).reshape(rows // 16, 2, 8, toks)
    low = disp[:, 0].reshape(rows // 2, toks).astype(BF16)
    high = disp[:, 1].reshape(rows // 2, toks).astype(BF16)
    recv = recv_ref[...]
    out = lax.dot_general(recv, low, FIRST, preferred_element_type=F32)[0:64, :]
    out = out + lax.dot_general(recv, high, FIRST, preferred_element_type=F32)[64:128, :]
    out_ref[...] = out.astype(BF16)


def per_device(tokens, out_grad, probs, expert_ids, w_gate, w_up, w_down):
    blocks = lax.axis_size("ep")
    experts = lax.axis_size("edp")
    toks, width = tokens.shape
    share = experts // blocks
    slots = blocks * CAP
    wide = w_gate.shape[1]
    hid = w_gate.shape[2]
    gate, up, down = w_gate[0], w_up[0], w_down[0]

    there = [
        (b * experts + j, (j // share) * experts + b * share + j % share)
        for b in range(blocks)
        for j in range(experts)
    ]
    back = [(d, s) for s, d in there]

    ids = expert_ids.T
    packed = jnp.concatenate(
        [tokens.T, out_grad.T, ids.astype(BF16), jnp.zeros((8, toks), BF16)], axis=0
    )
    packed = lax.ppermute(packed, ("ep", "edp"), there)

    rank = jnp.full((1,), lax.axis_index(("ep", "edp")), jnp.int32)

    def slot_weights(*refs):
        weight_body(experts, *refs)

    weight = pl.pallas_call(
        slot_weights,
        out_shape=arr((CAP, toks), F32),
        in_specs=[pl.BlockSpec(memory_space=pltpu.SMEM)]
        + [pl.BlockSpec(memory_space=pltpu.VMEM)] * 2
        + [pl.BlockSpec(memory_space=pl.ANY)] * 3,
        cost_estimate=pl.CostEstimate(flops=10**5, bytes_accessed=10**4, transcendentals=0),
    )(rank, ids, probs.T, gate, up, down)

    packed, weight = lax.optimization_barrier((packed, weight))

    def body(*refs):
        dispatch_body(experts, *refs)

    sent, disp = call(
        body,
        (arr((experts * CAP, 2 * width)), arr((experts * CAP, toks))),
        2 * experts * CAP * toks * 2 * width,
        6 * 10**5,
        packed,
    )
    recv = lax.all_to_all(
        sent.reshape(experts, CAP, 2 * width), "edp", split_axis=0, concat_axis=0, tiled=True
    ).reshape(experts * CAP, 2 * width)

    part, x_s, y_s = pl.pallas_call(
        project_body,
        out_shape=(arr((slots, 3 * hid)), arr((slots, wide)), arr((slots, wide))),
        in_specs=[pl.BlockSpec(memory_space=pltpu.VMEM)]
        + [pl.BlockSpec(memory_space=pl.ANY)] * 3,
        scratch_shapes=[
            pltpu.VMEM((wide, hid), BF16),
            pltpu.VMEM((wide, hid), BF16),
            pltpu.VMEM((hid, wide), BF16),
            pltpu.SemaphoreType.DMA((3,)),
        ],
        compiler_params=pltpu.CompilerParams(vmem_limit_bytes=40 * 1024 * 1024),
        cost_estimate=pl.CostEstimate(
            flops=6 * slots * wide * hid, bytes_accessed=4 * 10**6, transcendentals=0
        ),
    )(recv, gate, up, down)
    parts = lax.all_to_all(
        part.reshape(blocks, CAP, 3 * hid), "ep", split_axis=0, concat_axis=0, tiled=True
    ).reshape(slots, 3 * hid)

    mine = call(hidden_body, arr((CAP, 3 * hid)), 10**6, 2 * 10**6, parts, weight)

    ring = blocks // 2

    def shifted(step):
        return [
            (
                b * experts + e,
                ((b // 2 + (step if e % 2 == 0 else -step)) % ring * 2 + b % 2) * experts + e,
            )
            for b in range(blocks)
            for e in range(experts)
        ]

    other = lax.ppermute(mine, "ep", [(b, b ^ 1) for b in range(blocks)])
    pair = jnp.concatenate([mine, other], axis=0)

    def passed(piece, step):
        return lax.ppermute(piece, ("ep", "edp"), shifted(step))

    right_two, left_two = passed(pair, 2), passed(pair, -2)
    right_on = passed(jnp.concatenate([right_two, pair], axis=0), 1)
    left_on = passed(jnp.concatenate([left_two, pair], axis=0), -1)
    steps = [(0,), (-2,), (2,), (-3, -1), (3, 1), (-4,)]
    pieces = [pair, right_two, left_two, right_on, left_on, passed(right_two, 2)]

    def slot_body(*refs):
        slot_grad_body(experts, steps, *refs)

    slot_grad, grads = pl.pallas_call(
        slot_body,
        out_shape=(arr((4 * slots // 2, 128)), arr((slots, 3 * hid))),
        in_specs=[pl.BlockSpec(memory_space=pltpu.SMEM)]
        + [pl.BlockSpec(memory_space=pltpu.VMEM)] * (len(pieces) + 2),
        compiler_params=pltpu.CompilerParams(vmem_limit_bytes=40 * 1024 * 1024),
        cost_estimate=pl.CostEstimate(
            flops=4 * slots * wide * hid, bytes_accessed=5 * 10**6, transcendentals=0
        ),
    )(rank, *pieces, gate, up)
    returned = lax.all_to_all(
        slot_grad.reshape(experts, 8, 128), "edp", split_axis=0, concat_axis=0, tiled=True
    ).reshape(experts * 8, 128)

    token_grad = call(
        combine_body, arr((width, toks)), 4 * experts * 8 * 128 * toks, 4 * 10**5, returned, disp
    )
    grads, token_grad = lax.optimization_barrier((grads, token_grad))
    grad_gate, grad_up, grad_down = call(
        weight_grads_body,
        (arr((wide, hid)), arr((wide, hid)), arr((hid, wide))),
        6 * slots * wide * hid,
        4 * 10**6,
        x_s,
        y_s,
        grads,
    )
    token_grad = lax.ppermute(token_grad, ("ep", "edp"), back).T
    return (token_grad, grad_gate[None], grad_up[None], grad_down[None])


def solution(mesh):
    placed = (
        P("ep", "edp"),
        P("ep", "edp"),
        P("ep", None),
        P("ep", None),
        P("edp", "ep", None),
        P("edp", "ep", None),
        P("edp", None, "ep"),
    )
    return jax.shard_map(
        per_device,
        mesh=mesh,
        in_specs=placed,
        out_specs=(
            P("ep", "edp"),
            P("edp", "ep", None),
            P("edp", "ep", None),
            P("edp", None, "ep"),
        ),
        check_vma=False,
    )
```

```python
import jax
import jax.numpy as jnp
from jax import lax
from jax.experimental import pallas as pl
from jax.experimental.pallas import tpu as pltpu
from jax.sharding import PartitionSpec as P

CAP = 16
BF16 = jnp.bfloat16
F32 = jnp.float32
LAST = (((1,), (1,)), ((), ()))
FIRST = (((0,), (0,)), ((), ()))


def call(body, outs, flops, moved, *args):
    return pl.pallas_call(
        body,
        out_shape=outs,
        compiler_params=pltpu.CompilerParams(vmem_limit_bytes=40 * 1024 * 1024),
        cost_estimate=pl.CostEstimate(flops=flops, bytes_accessed=moved, transcendentals=0),
    )(*args)


def arr(shape, dtype=BF16):
    return jax.ShapeDtypeStruct(shape, dtype)


def before(toks):
    row = lax.broadcasted_iota(jnp.int32, (toks, toks), 0)
    col = lax.broadcasted_iota(jnp.int32, (toks, toks), 1)
    return jnp.where(row < col, 1.0, 0.0).astype(BF16)


def dispatch_body(experts, packed_ref, sent_ref, disp_ref):
    feats = packed_ref[0:128, :]
    ids = packed_ref[128:144, :].astype(F32)
    toks = ids.shape[1]
    names = lax.broadcasted_iota(jnp.int32, (experts, toks), 0).astype(F32)
    mask = jnp.zeros((experts, toks), F32)
    for k in range(8):
        mask = mask + jnp.where(ids[k : k + 1, :] == names, 1.0, 0.0)
    rank = jnp.dot(mask.astype(BF16), before(toks), preferred_element_type=F32)
    slot = jnp.where(mask > 0.0, rank, -1.0)
    place = lax.broadcasted_iota(jnp.int32, (CAP, toks), 0).astype(F32)
    for e in range(experts):
        disp_ref[e * CAP : (e + 1) * CAP, :] = jnp.where(
            slot[e : e + 1, :] == place, 1.0, 0.0
        ).astype(BF16)
    sent_ref[...] = lax.dot_general(
        disp_ref[...], feats, LAST, preferred_element_type=F32
    ).astype(BF16)


def weight_body(experts, place_ref, ids_ref, probs_ref, gate_ref, up_ref, down_ref, out_ref):
    mine = jnp.where(ids_ref[...] == lax.rem(place_ref[0], experts), 1.0, 0.0)
    toks = mine.shape[1]
    mask = jnp.sum(mine, axis=0, keepdims=True)
    weight = jnp.sum(mine * probs_ref[...], axis=0, keepdims=True)
    rank = jnp.dot(
        jnp.broadcast_to(mask, (16, toks)).astype(BF16), before(toks), preferred_element_type=F32
    )
    place = lax.broadcasted_iota(jnp.int32, (CAP, toks), 0).astype(F32)
    hit = (rank == place) & (jnp.broadcast_to(mask, (CAP, toks)) > 0.0)
    picked = jnp.where(hit, jnp.broadcast_to(weight, (CAP, toks)), 0.0)
    out_ref[...] = jnp.broadcast_to(jnp.sum(picked, axis=1, keepdims=True), (CAP, toks))


def project_body(
    recv_ref, gate_hbm, up_hbm, down_hbm, part_ref, x_ref, y_ref, gate_ref, up_ref, down_ref, sems
):
    loads = [
        pltpu.make_async_copy(src, dst, sems.at[k])
        for k, (src, dst) in enumerate(
            ((gate_hbm, gate_ref), (up_hbm, up_ref), (down_hbm, down_ref))
        )
    ]
    for load in loads:
        load.start()
    rows = recv_ref.shape[0] // 4
    recv = recv_ref[...].reshape(rows // CAP, 4, CAP, 128)
    for q in range(4):
        block = recv[:, q].reshape(rows, 128)
        x_ref[:, q * 64 : (q + 1) * 64] = block[:, :64]
        y_ref[:, q * 64 : (q + 1) * 64] = block[:, 64:]
    x = x_ref[...]
    y = y_ref[...]
    hid = gate_ref.shape[1]
    loads[0].wait()
    part_ref[:, 0:hid] = jnp.dot(x, gate_ref[...], preferred_element_type=F32).astype(BF16)
    loads[1].wait()
    part_ref[:, hid : 2 * hid] = jnp.dot(x, up_ref[...], preferred_element_type=F32).astype(BF16)
    loads[2].wait()
    part_ref[:, 2 * hid : 3 * hid] = lax.dot_general(
        y, down_ref[...], LAST, preferred_element_type=F32
    ).astype(BF16)


def hidden_body(parts_ref, weight_ref, grads_ref):
    peers = parts_ref.shape[0] // CAP
    hid = parts_ref.shape[1] // 3
    total = parts_ref[0:CAP, :].astype(F32)
    for s in range(1, peers):
        total = total + parts_ref[s * CAP : (s + 1) * CAP, :].astype(F32)
    gate = total[:, 0:hid]
    up = total[:, hid : 2 * hid]
    back = total[:, 2 * hid : 3 * hid]
    weight = weight_ref[:, 0:1]
    sig = jax.nn.sigmoid(gate)
    silu = gate * sig
    hidden_grad = weight * back
    hidden_weighted = (weight * silu * up).astype(BF16)
    up_grad = (hidden_grad * silu).astype(BF16)
    gate_grad = (hidden_grad * up * sig * (1.0 + gate * (1.0 - sig))).astype(BF16)
    grads_ref[:, 0:hid] = gate_grad
    grads_ref[:, hid : 2 * hid] = up_grad
    grads_ref[:, 2 * hid : 3 * hid] = hidden_weighted


def slot_grad_body(experts, steps, place_ref, *refs):
    pieces, (gate_ref, up_ref, out_ref, grads_ref) = refs[:-4], refs[-4:]
    hid = gate_ref.shape[1]
    ring = sum(len(held) for held in steps)
    spot = lax.div(place_ref[0], 2 * experts)
    side = lax.rem(lax.div(place_ref[0], experts), 2)
    way = 1 - 2 * lax.rem(place_ref[0], 2)
    for held, piece_ref in zip(steps, pieces, strict=True):
        for at, step in enumerate(held):
            pair = 2 * CAP * lax.rem(spot + step * way + ring, ring)
            for half, z in ((0, side), (1, 1 - side)):
                row = pl.multiple_of(pair + CAP * z, CAP)
                low = (2 * at + half) * CAP
                grads_ref[pl.ds(row, CAP), :] = piece_ref[low : low + CAP, :]
    slot_grad = lax.dot_general(
        grads_ref[:, 0:hid], gate_ref[...], LAST, preferred_element_type=F32
    ) + lax.dot_general(
        grads_ref[:, hid : 2 * hid], up_ref[...], LAST, preferred_element_type=F32
    )
    blocks = slot_grad.shape[0] // CAP
    wide = slot_grad.shape[1]
    pairs = slot_grad.reshape(blocks, 2, 8, wide)
    low, high = pairs[:, 0], pairs[:, 1]
    shares = []
    for q in range(4):
        cols = slice(q * 64, (q + 1) * 64)
        shares.append(jnp.concatenate([low[:, :, cols], high[:, :, cols]], axis=2)[:, None])
    out = jnp.concatenate(shares, axis=1).reshape(4 * 8 * blocks, 128)
    out_ref[...] = out.astype(BF16)


def weight_grads_body(x_ref, y_ref, grads_ref, gate_ref, up_ref, down_ref):
    hid = gate_ref.shape[1]
    x = x_ref[...]
    gate_ref[...] = lax.dot_general(
        x, grads_ref[:, 0:hid], FIRST, preferred_element_type=F32
    ).astype(BF16)
    up_ref[...] = lax.dot_general(
        x, grads_ref[:, hid : 2 * hid], FIRST, preferred_element_type=F32
    ).astype(BF16)
    down_ref[...] = lax.dot_general(
        grads_ref[:, 2 * hid : 3 * hid], y_ref[...], FIRST, preferred_element_type=F32
    ).astype(BF16)


def combine_body(recv_ref, disp_ref, out_ref):
    rows = disp_ref.shape[0]
    toks = disp_ref.shape[1]
    disp = disp_ref[...].astype(F32).reshape(rows // 16, 2, 8, toks)
    low = disp[:, 0].reshape(rows // 2, toks).astype(BF16)
    high = disp[:, 1].reshape(rows // 2, toks).astype(BF16)
    recv = recv_ref[...]
    out = lax.dot_general(recv, low, FIRST, preferred_element_type=F32)[0:64, :]
    out = out + lax.dot_general(recv, high, FIRST, preferred_element_type=F32)[64:128, :]
    out_ref[...] = out.astype(BF16)


def per_device(tokens, out_grad, probs, expert_ids, w_gate, w_up, w_down):
    blocks = lax.axis_size("ep")
    experts = lax.axis_size("edp")
    toks, width = tokens.shape
    share = experts // blocks
    slots = blocks * CAP
    wide = w_gate.shape[1]
    hid = w_gate.shape[2]
    gate, up, down = w_gate[0], w_up[0], w_down[0]

    there = [
        (b * experts + j, (j // share) * experts + b * share + j % share)
        for b in range(blocks)
        for j in range(experts)
    ]
    back = [(d, s) for s, d in there]

    ids = expert_ids.T
    packed = jnp.concatenate(
        [tokens.T, out_grad.T, ids.astype(BF16), jnp.zeros((8, toks), BF16)], axis=0
    )
    packed = lax.ppermute(packed, ("ep", "edp"), there)

    rank = jnp.full((1,), lax.axis_index(("ep", "edp")), jnp.int32)

    def slot_weights(*refs):
        weight_body(experts, *refs)

    weight = pl.pallas_call(
        slot_weights,
        out_shape=arr((CAP, toks), F32),
        in_specs=[pl.BlockSpec(memory_space=pltpu.SMEM)]
        + [pl.BlockSpec(memory_space=pltpu.VMEM)] * 2
        + [pl.BlockSpec(memory_space=pl.ANY)] * 3,
        cost_estimate=pl.CostEstimate(flops=10**5, bytes_accessed=10**4, transcendentals=0),
    )(rank, ids, probs.T, gate, up, down)

    packed, weight = lax.optimization_barrier((packed, weight))

    def body(*refs):
        dispatch_body(experts, *refs)

    sent, disp = call(
        body,
        (arr((experts * CAP, 2 * width)), arr((experts * CAP, toks))),
        2 * experts * CAP * toks * 2 * width,
        6 * 10**5,
        packed,
    )
    recv = lax.all_to_all(
        sent.reshape(experts, CAP, 2 * width), "edp", split_axis=0, concat_axis=0, tiled=True
    ).reshape(experts * CAP, 2 * width)

    part, x_s, y_s = pl.pallas_call(
        project_body,
        out_shape=(arr((slots, 3 * hid)), arr((slots, wide)), arr((slots, wide))),
        in_specs=[pl.BlockSpec(memory_space=pltpu.VMEM)]
        + [pl.BlockSpec(memory_space=pl.ANY)] * 3,
        scratch_shapes=[
            pltpu.VMEM((wide, hid), BF16),
            pltpu.VMEM((wide, hid), BF16),
            pltpu.VMEM((hid, wide), BF16),
            pltpu.SemaphoreType.DMA((3,)),
        ],
        compiler_params=pltpu.CompilerParams(vmem_limit_bytes=40 * 1024 * 1024),
        cost_estimate=pl.CostEstimate(
            flops=6 * slots * wide * hid, bytes_accessed=4 * 10**6, transcendentals=0
        ),
    )(recv, gate, up, down)
    parts = lax.all_to_all(
        part.reshape(blocks, CAP, 3 * hid), "ep", split_axis=0, concat_axis=0, tiled=True
    ).reshape(slots, 3 * hid)

    mine = call(hidden_body, arr((CAP, 3 * hid)), 10**6, 2 * 10**6, parts, weight)

    ring = blocks // 2

    def shifted(step):
        return [
            (
                b * experts + e,
                ((b // 2 + (step if e % 2 == 0 else -step)) % ring * 2 + b % 2) * experts + e,
            )
            for b in range(blocks)
            for e in range(experts)
        ]

    other = lax.ppermute(mine, "ep", [(b, b ^ 1) for b in range(blocks)])
    pair = jnp.concatenate([mine, other], axis=0)

    def passed(piece, step):
        return lax.ppermute(piece, ("ep", "edp"), shifted(step))

    right_two, left_two = passed(pair, 2), passed(pair, -2)
    right_one, left_one = passed(pair, 1), passed(pair, -1)
    right_three, left_three = passed(right_two, 1), passed(left_two, -1)
    steps = [(0,), (-2,), (2,), (-1,), (1,), (-3,), (3,), (-4,)]
    pieces = [pair, right_two, left_two, right_one, left_one, right_three, left_three]
    pieces.append(passed(right_two, 2))

    def slot_body(*refs):
        slot_grad_body(experts, steps, *refs)

    slot_grad, grads = pl.pallas_call(
        slot_body,
        out_shape=(arr((4 * slots // 2, 128)), arr((slots, 3 * hid))),
        in_specs=[pl.BlockSpec(memory_space=pltpu.SMEM)]
        + [pl.BlockSpec(memory_space=pltpu.VMEM)] * (len(pieces) + 2),
        compiler_params=pltpu.CompilerParams(vmem_limit_bytes=40 * 1024 * 1024),
        cost_estimate=pl.CostEstimate(
            flops=4 * slots * wide * hid, bytes_accessed=5 * 10**6, transcendentals=0
        ),
    )(rank, *pieces, gate, up)
    returned = lax.all_to_all(
        slot_grad.reshape(experts, 8, 128), "edp", split_axis=0, concat_axis=0, tiled=True
    ).reshape(experts * 8, 128)

    token_grad = call(
        combine_body, arr((width, toks)), 4 * experts * 8 * 128 * toks, 4 * 10**5, returned, disp
    )
    grads, token_grad = lax.optimization_barrier((grads, token_grad))
    grad_gate, grad_up, grad_down = call(
        weight_grads_body,
        (arr((wide, hid)), arr((wide, hid)), arr((hid, wide))),
        6 * slots * wide * hid,
        4 * 10**6,
        x_s,
        y_s,
        grads,
    )
    token_grad = lax.ppermute(token_grad, ("ep", "edp"), back).T
    return (token_grad, grad_gate[None], grad_up[None], grad_down[None])


def solution(mesh):
    placed = (
        P("ep", "edp"),
        P("ep", "edp"),
        P("ep", None),
        P("ep", None),
        P("edp", "ep", None),
        P("edp", "ep", None),
        P("edp", None, "ep"),
    )
    return jax.shard_map(
        per_device,
        mesh=mesh,
        in_specs=placed,
        out_specs=(
            P("ep", "edp"),
            P("edp", "ep", None),
            P("edp", "ep", None),
            P("edp", None, "ep"),
        ),
        check_vma=False,
    )
```

```python
import jax
import jax.numpy as jnp
from jax import lax
from jax.experimental import pallas as pl
from jax.experimental.pallas import tpu as pltpu
from jax.sharding import PartitionSpec as P

CAP = 16
BF16 = jnp.bfloat16
F32 = jnp.float32
LAST = (((1,), (1,)), ((), ()))
FIRST = (((0,), (0,)), ((), ()))


def call(body, outs, flops, moved, *args):
    return pl.pallas_call(
        body,
        out_shape=outs,
        compiler_params=pltpu.CompilerParams(vmem_limit_bytes=40 * 1024 * 1024),
        cost_estimate=pl.CostEstimate(flops=flops, bytes_accessed=moved, transcendentals=0),
    )(*args)


def arr(shape, dtype=BF16):
    return jax.ShapeDtypeStruct(shape, dtype)


def before(toks):
    row = lax.broadcasted_iota(jnp.int32, (toks, toks), 0)
    col = lax.broadcasted_iota(jnp.int32, (toks, toks), 1)
    return jnp.where(row < col, 1.0, 0.0).astype(BF16)


def dispatch_body(experts, packed_ref, sent_ref, disp_ref):
    feats = packed_ref[0:128, :]
    ids = packed_ref[128:144, :].astype(F32)
    toks = ids.shape[1]
    names = lax.broadcasted_iota(jnp.int32, (experts, toks), 0).astype(F32)
    mask = jnp.zeros((experts, toks), F32)
    for k in range(8):
        mask = mask + jnp.where(ids[k : k + 1, :] == names, 1.0, 0.0)
    rank = jnp.dot(mask.astype(BF16), before(toks), preferred_element_type=F32)
    slot = jnp.where(mask > 0.0, rank, -1.0)
    place = lax.broadcasted_iota(jnp.int32, (CAP, toks), 0).astype(F32)
    for e in range(experts):
        disp_ref[e * CAP : (e + 1) * CAP, :] = jnp.where(
            slot[e : e + 1, :] == place, 1.0, 0.0
        ).astype(BF16)
    sent_ref[...] = lax.dot_general(
        disp_ref[...], feats, LAST, preferred_element_type=F32
    ).astype(BF16)


def weight_body(experts, place_ref, ids_ref, probs_ref, gate_ref, up_ref, down_ref, out_ref):
    mine = jnp.where(ids_ref[...] == lax.rem(place_ref[0], experts), 1.0, 0.0)
    toks = mine.shape[1]
    mask = jnp.sum(mine, axis=0, keepdims=True)
    weight = jnp.sum(mine * probs_ref[...], axis=0, keepdims=True)
    rank = jnp.dot(
        jnp.broadcast_to(mask, (16, toks)).astype(BF16), before(toks), preferred_element_type=F32
    )
    place = lax.broadcasted_iota(jnp.int32, (CAP, toks), 0).astype(F32)
    hit = (rank == place) & (jnp.broadcast_to(mask, (CAP, toks)) > 0.0)
    picked = jnp.where(hit, jnp.broadcast_to(weight, (CAP, toks)), 0.0)
    out_ref[...] = jnp.broadcast_to(jnp.sum(picked, axis=1, keepdims=True), (CAP, toks))


def project_body(
    recv_ref, gate_hbm, up_hbm, down_hbm, part_ref, x_ref, y_ref, gate_ref, up_ref, down_ref, sems
):
    loads = [
        pltpu.make_async_copy(src, dst, sems.at[k])
        for k, (src, dst) in enumerate(
            ((gate_hbm, gate_ref), (up_hbm, up_ref), (down_hbm, down_ref))
        )
    ]
    for load in loads:
        load.start()
    rows = recv_ref.shape[0] // 4
    recv = recv_ref[...].reshape(rows // CAP, 4, CAP, 128)
    for q in range(4):
        block = recv[:, q].reshape(rows, 128)
        x_ref[:, q * 64 : (q + 1) * 64] = block[:, :64]
        y_ref[:, q * 64 : (q + 1) * 64] = block[:, 64:]
    x = x_ref[...]
    y = y_ref[...]
    hid = gate_ref.shape[1]
    loads[0].wait()
    part_ref[:, 0:hid] = jnp.dot(x, gate_ref[...], preferred_element_type=F32).astype(BF16)
    loads[1].wait()
    part_ref[:, hid : 2 * hid] = jnp.dot(x, up_ref[...], preferred_element_type=F32).astype(BF16)
    loads[2].wait()
    part_ref[:, 2 * hid : 3 * hid] = lax.dot_general(
        y, down_ref[...], LAST, preferred_element_type=F32
    ).astype(BF16)


def hidden_body(parts_ref, weight_ref, grads_ref):
    peers = parts_ref.shape[0] // CAP
    hid = parts_ref.shape[1] // 3
    total = parts_ref[0:CAP, :].astype(F32)
    for s in range(1, peers):
        total = total + parts_ref[s * CAP : (s + 1) * CAP, :].astype(F32)
    gate = total[:, 0:hid]
    up = total[:, hid : 2 * hid]
    back = total[:, 2 * hid : 3 * hid]
    weight = weight_ref[:, 0:1]
    sig = jax.nn.sigmoid(gate)
    silu = gate * sig
    hidden_grad = weight * back
    hidden_weighted = (weight * silu * up).astype(BF16)
    up_grad = (hidden_grad * silu).astype(BF16)
    gate_grad = (hidden_grad * up * sig * (1.0 + gate * (1.0 - sig))).astype(BF16)
    grads_ref[:, 0:hid] = gate_grad
    grads_ref[:, hid : 2 * hid] = up_grad
    grads_ref[:, 2 * hid : 3 * hid] = hidden_weighted


def slot_grad_body(experts, steps, place_ref, *refs):
    pieces, (gate_ref, up_ref, out_ref, grads_ref) = refs[:-4], refs[-4:]
    hid = gate_ref.shape[1]
    ring = sum(len(held) for held in steps)
    spot = lax.div(place_ref[0], 2 * experts)
    side = lax.rem(lax.div(place_ref[0], experts), 2)
    for held, piece_ref in zip(steps, pieces, strict=True):
        for at, step in enumerate(held):
            pair = 2 * CAP * lax.rem(spot + step + ring, ring)
            for half, z in ((0, side), (1, 1 - side)):
                row = pl.multiple_of(pair + CAP * z, CAP)
                low = (2 * at + half) * CAP
                grads_ref[pl.ds(row, CAP), :] = piece_ref[low : low + CAP, :]
    slot_grad = lax.dot_general(
        grads_ref[:, 0:hid], gate_ref[...], LAST, preferred_element_type=F32
    ) + lax.dot_general(
        grads_ref[:, hid : 2 * hid], up_ref[...], LAST, preferred_element_type=F32
    )
    blocks = slot_grad.shape[0] // CAP
    wide = slot_grad.shape[1]
    pairs = slot_grad.reshape(blocks, 2, 8, wide)
    low, high = pairs[:, 0], pairs[:, 1]
    shares = []
    for q in range(4):
        cols = slice(q * 64, (q + 1) * 64)
        shares.append(jnp.concatenate([low[:, :, cols], high[:, :, cols]], axis=2)[:, None])
    out = jnp.concatenate(shares, axis=1).reshape(4 * 8 * blocks, 128)
    out_ref[...] = out.astype(BF16)


def weight_grads_body(x_ref, y_ref, grads_ref, gate_ref, up_ref, down_ref):
    hid = gate_ref.shape[1]
    x = x_ref[...]
    gate_ref[...] = lax.dot_general(
        x, grads_ref[:, 0:hid], FIRST, preferred_element_type=F32
    ).astype(BF16)
    up_ref[...] = lax.dot_general(
        x, grads_ref[:, hid : 2 * hid], FIRST, preferred_element_type=F32
    ).astype(BF16)
    down_ref[...] = lax.dot_general(
        grads_ref[:, 2 * hid : 3 * hid], y_ref[...], FIRST, preferred_element_type=F32
    ).astype(BF16)


def combine_body(recv_ref, disp_ref, out_ref):
    rows = disp_ref.shape[0]
    toks = disp_ref.shape[1]
    disp = disp_ref[...].astype(F32).reshape(rows // 16, 2, 8, toks)
    low = disp[:, 0].reshape(rows // 2, toks).astype(BF16)
    high = disp[:, 1].reshape(rows // 2, toks).astype(BF16)
    recv = recv_ref[...]
    out = lax.dot_general(recv, low, FIRST, preferred_element_type=F32)[0:64, :]
    out = out + lax.dot_general(recv, high, FIRST, preferred_element_type=F32)[64:128, :]
    out_ref[...] = out.astype(BF16)


def per_device(tokens, out_grad, probs, expert_ids, w_gate, w_up, w_down):
    blocks = lax.axis_size("ep")
    experts = lax.axis_size("edp")
    toks, width = tokens.shape
    share = experts // blocks
    slots = blocks * CAP
    wide = w_gate.shape[1]
    hid = w_gate.shape[2]
    gate, up, down = w_gate[0], w_up[0], w_down[0]

    there = [
        (b * experts + j, (j // share) * experts + b * share + j % share)
        for b in range(blocks)
        for j in range(experts)
    ]
    back = [(d, s) for s, d in there]

    ids = expert_ids.T
    packed = jnp.concatenate(
        [tokens.T, out_grad.T, ids.astype(BF16), jnp.zeros((8, toks), BF16)], axis=0
    )
    packed = lax.ppermute(packed, ("ep", "edp"), there)

    rank = jnp.full((1,), lax.axis_index(("ep", "edp")), jnp.int32)

    def slot_weights(*refs):
        weight_body(experts, *refs)

    weight = pl.pallas_call(
        slot_weights,
        out_shape=arr((CAP, toks), F32),
        in_specs=[pl.BlockSpec(memory_space=pltpu.SMEM)]
        + [pl.BlockSpec(memory_space=pltpu.VMEM)] * 2
        + [pl.BlockSpec(memory_space=pl.ANY)] * 3,
        cost_estimate=pl.CostEstimate(flops=10**5, bytes_accessed=10**4, transcendentals=0),
    )(rank, ids, probs.T, gate, up, down)

    packed, weight = lax.optimization_barrier((packed, weight))

    def body(*refs):
        dispatch_body(experts, *refs)

    sent, disp = call(
        body,
        (arr((experts * CAP, 2 * width)), arr((experts * CAP, toks))),
        2 * experts * CAP * toks * 2 * width,
        6 * 10**5,
        packed,
    )
    recv = lax.all_to_all(
        sent.reshape(experts, CAP, 2 * width), "edp", split_axis=0, concat_axis=0, tiled=True
    ).reshape(experts * CAP, 2 * width)

    part, x_s, y_s = pl.pallas_call(
        project_body,
        out_shape=(arr((slots, 3 * hid)), arr((slots, wide)), arr((slots, wide))),
        in_specs=[pl.BlockSpec(memory_space=pltpu.VMEM)]
        + [pl.BlockSpec(memory_space=pl.ANY)] * 3,
        scratch_shapes=[
            pltpu.VMEM((wide, hid), BF16),
            pltpu.VMEM((wide, hid), BF16),
            pltpu.VMEM((hid, wide), BF16),
            pltpu.SemaphoreType.DMA((3,)),
        ],
        compiler_params=pltpu.CompilerParams(vmem_limit_bytes=40 * 1024 * 1024),
        cost_estimate=pl.CostEstimate(
            flops=6 * slots * wide * hid, bytes_accessed=4 * 10**6, transcendentals=0
        ),
    )(recv, gate, up, down)
    parts = lax.all_to_all(
        part.reshape(blocks, CAP, 3 * hid), "ep", split_axis=0, concat_axis=0, tiled=True
    ).reshape(slots, 3 * hid)

    mine = call(hidden_body, arr((CAP, 3 * hid)), 10**6, 2 * 10**6, parts, weight)

    ring = blocks // 2

    def shifted(step):
        return [
            (
                b * experts + e,
                ((b // 2 + step) % ring * 2 + b % 2) * experts + e,
            )
            for b in range(blocks)
            for e in range(experts)
        ]

    other = lax.ppermute(mine, "ep", [(b, b ^ 1) for b in range(blocks)])
    pair = jnp.concatenate([mine, other], axis=0)

    def passed(piece, step):
        return lax.ppermute(piece, ("ep", "edp"), shifted(step))

    right_two, left_two = passed(pair, 2), passed(pair, -2)
    right_one, left_one = passed(pair, 1), passed(pair, -1)
    right_three, left_three = passed(right_two, 1), passed(left_two, -1)
    steps = [(0,), (-2,), (2,), (-1,), (1,), (-3,), (3,), (-4,)]
    pieces = [pair, right_two, left_two, right_one, left_one, right_three, left_three]
    pieces.append(passed(right_two, 2))

    def slot_body(*refs):
        slot_grad_body(experts, steps, *refs)

    slot_grad, grads = pl.pallas_call(
        slot_body,
        out_shape=(arr((4 * slots // 2, 128)), arr((slots, 3 * hid))),
        in_specs=[pl.BlockSpec(memory_space=pltpu.SMEM)]
        + [pl.BlockSpec(memory_space=pltpu.VMEM)] * (len(pieces) + 2),
        compiler_params=pltpu.CompilerParams(vmem_limit_bytes=40 * 1024 * 1024),
        cost_estimate=pl.CostEstimate(
            flops=4 * slots * wide * hid, bytes_accessed=5 * 10**6, transcendentals=0
        ),
    )(rank, *pieces, gate, up)
    returned = lax.all_to_all(
        slot_grad.reshape(experts, 8, 128), "edp", split_axis=0, concat_axis=0, tiled=True
    ).reshape(experts * 8, 128)

    token_grad = call(
        combine_body, arr((width, toks)), 4 * experts * 8 * 128 * toks, 4 * 10**5, returned, disp
    )
    grads, token_grad = lax.optimization_barrier((grads, token_grad))
    grad_gate, grad_up, grad_down = call(
        weight_grads_body,
        (arr((wide, hid)), arr((wide, hid)), arr((hid, wide))),
        6 * slots * wide * hid,
        4 * 10**6,
        x_s,
        y_s,
        grads,
    )
    token_grad = lax.ppermute(token_grad, ("ep", "edp"), back).T
    return (token_grad, grad_gate[None], grad_up[None], grad_down[None])


def solution(mesh):
    placed = (
        P("ep", "edp"),
        P("ep", "edp"),
        P("ep", None),
        P("ep", None),
        P("edp", "ep", None),
        P("edp", "ep", None),
        P("edp", None, "ep"),
    )
    return jax.shard_map(
        per_device,
        mesh=mesh,
        in_specs=placed,
        out_specs=(
            P("ep", "edp"),
            P("edp", "ep", None),
            P("edp", "ep", None),
            P("edp", None, "ep"),
        ),
        check_vma=False,
    )
```
